32 devices in a mesh: grp: 4 (over x, core), blk: 8 (over z, y).
Axes of the slice: x: 2, y: 2, z: 4, core: 2. Of those that a mesh axis runs over, the one named last changes fastest.
Arguments:
- held: float32 [4, 3, 90, 4096], P('grp', None, None, 'blk'), may hold values from -6 to 6
- neighbours: int32 [6, 4096], P(None, 'blk'), may hold values from 0 to 767
- send_rows: int32 [2, 1024], P(None, 'blk'), may hold values from 0 to 511
- diffusion: float32 [6, 4096], P(None, 'blk'), may hold values from 0.02 to 0.12
- transport: float32 [6, 4096], P(None, 'blk'), may hold values from -0.06 to 0.06
- w_in: bfloat16 [512, 270], replicated, may hold values from -0.375 to 0.375
- b_in: float32 [512], replicated, may hold values from -3 to 3
- w_mid: bfloat16 [512, 512], replicated, may hold values from -0.25 to 0.25
- b_mid: float32 [512], replicated, may hold values from -3 to 3
- w_out: bfloat16 [90, 512], replicated, may hold values from -0.25 to 0.25
- b_out: float32 [90], replicated, may hold values from -3 to 3
Outputs:
- held_new: float32 [4, 3, 90, 4096], P('grp', None, None, 'blk')
The draws below stay inside these ranges and needn't reach their ends.
All inputs are finite; a program needn't handle non-finite values.
Results may differ from the reference program's by a relative error of at most 0.0017.
Values may be sent and summed in bfloat16 or wider, within the bound.
No kernel may reach another device: no remote copies, remote signals or barrier semaphores. Data moves between devices by JAX's collectives and lax.ppermute only.
A program may use at most 64 MiB of HBM per device.

```python
import math
import jax
import jax.numpy as jnp
from jax import lax

LEV = 90
FIELDS = 3
HID = 512
CELLS = 512
FEAT = 270
HALO = 128
N_GRP = 4
N_BLK = 8


def set_ends(array, rng, smallest, largest):
    extent = array.shape
    index_at = [jax.random.randint(jax.random.fold_in(rng, axis), (), 0, extent[axis]) for axis in range(len(extent))]
    array = array.at[tuple(index_at)].set(smallest)
    longest = extent.index(max(extent))
    index_at[longest] = (index_at[longest] + 1) % extent[longest]
    return array.at[tuple(index_at)].set(largest)


def block_levels(own_key, dims, pieces, smallest, largest):
    loudness, own = 1.0, jax.random.fold_in(own_key, 6)
    for dim, blocks in pieces:
        draws = jnp.exp(jax.random.uniform(jax.random.fold_in(own, dim), (blocks,), jnp.float32, smallest / len(pieces), largest / len(pieces)))
        loudness = loudness * jnp.repeat(draws, dims[dim] // blocks).reshape([-1 if axis == dim else 1 for axis in range(len(dims))])
    return loudness


def noise(own_key, dims, width, most, split=(), dtype=jnp.bfloat16):
    drawn = jax.random.normal(own_key, dims, jnp.float32) * width
    if len(split) > 0:
        drawn = block_levels(own_key, dims, split, -0.22, 0.18) * drawn
    return jnp.clip(drawn, min=-most, max=most).astype(dtype)


def setup_inputs(seed: int = 0) -> dict:
    arg_keys = jax.random.split(jax.random.key(seed), 12)
    return {
        "held": noise(arg_keys[0], (N_GRP, FIELDS, LEV, N_BLK * CELLS), 1.0, 6.0, ((0, 4), (3, 8)), jnp.float32),
        "neighbours": set_ends(jax.random.randint(arg_keys[1], (6, N_BLK * CELLS), 0, CELLS + 2 * HALO), jax.random.fold_in(arg_keys[1], 1), 0, (CELLS + 2 * HALO) - 1).astype(jnp.int32),
        "send_rows": set_ends(jax.random.randint(arg_keys[2], (2, N_BLK * HALO), 0, CELLS), jax.random.fold_in(arg_keys[2], 1), 0, CELLS - 1).astype(jnp.int32),
        "diffusion": jnp.clip(jnp.exp(math.log(0.12) - 1.7917595 * jax.random.uniform(arg_keys[3], (6, N_BLK * CELLS), jnp.float32) ** block_levels(arg_keys[3], (6, N_BLK * CELLS), ((1, 8),), -0.2, 0.2)), 0.02, 0.12),
        "transport": jnp.clip(jax.random.uniform(arg_keys[4], (6, N_BLK * CELLS), jnp.float32, -0.06, 0.06) * block_levels(arg_keys[4], (6, N_BLK * CELLS), ((1, 8),), -0.4, 0.0), -0.06, 0.06),
        "w_in": noise(arg_keys[5], (HID, FEAT), FEAT ** -0.5, 0.375),
        "b_in": noise(arg_keys[6], (HID,), 0.5, 3.0, (), jnp.float32),
        "w_mid": noise(arg_keys[7], (HID, HID), HID ** -0.5, 0.25),
        "b_mid": noise(arg_keys[8], (HID,), 0.5, 3.0, (), jnp.float32),
        "w_out": noise(arg_keys[9], (LEV, HID), HID ** -0.5, 0.25),
        "b_out": noise(arg_keys[10], (LEV,), 0.5, 3.0, (), jnp.float32),
    }


heat_gain = 0.5


def network(u, w_in, b_in, w_mid, b_mid, w_out, b_out):
    feats = u.reshape(FEAT, u.shape[-1]).astype(jnp.bfloat16)
    first = jnp.dot(w_in, feats, preferred_element_type=jnp.float32) + b_in[:, None]
    first = jax.nn.silu(first).astype(jnp.bfloat16)
    second = jnp.dot(w_mid, first, preferred_element_type=jnp.float32) + b_mid[:, None]
    second = jax.nn.silu(second).astype(jnp.bfloat16)
    return jnp.dot(w_out, second, preferred_element_type=jnp.float32) + b_out[:, None]


def advance(u, heat, neighbours, send_rows, diffusion, transport):
    blocks = u.reshape(FIELDS, LEV, N_BLK, CELLS)
    lists = send_rows.reshape(2, N_BLK, HALO)
    to_lower = jnp.take_along_axis(blocks, lists[0][None, None], axis=3)
    to_upper = jnp.take_along_axis(blocks, lists[1][None, None], axis=3)
    from_lower = jnp.roll(to_upper, 1, axis=2)
    from_upper = jnp.roll(to_lower, -1, axis=2)
    ext = jnp.concatenate((blocks, from_lower, from_upper), axis=3)
    near_idx = neighbours.reshape(6, N_BLK, CELLS)
    coef_d = diffusion.reshape(6, N_BLK, CELLS)
    coef_t = transport.reshape(6, N_BLK, CELLS)
    total = jnp.zeros_like(blocks)
    for edge in range(6):
        near = jnp.take_along_axis(ext, near_idx[edge][None, None], axis=3)
        total = total + coef_d[edge] * (near - blocks) - 0.5 * coef_t[edge] * (near + blocks)
    moved = blocks + total
    moved = moved.at[0].add(heat_gain * heat.reshape(LEV, N_BLK, CELLS))
    return moved.reshape(FIELDS, LEV, N_BLK * CELLS)


def reference(held, neighbours, send_rows, diffusion, transport, w_in, b_in, w_mid, b_mid, w_out, b_out):
    quarter = N_GRP // 4
    radiat = held[:quarter]
    state0 = held[quarter:]
    heat0 = jnp.transpose(radiat, (1, 0, 2, 3)).reshape(3 * quarter, LEV, N_BLK * CELLS)
    weights = (w_in, b_in, w_mid, b_mid, w_out, b_out)

    def heat_all(state):
        return lax.map(lambda u: network(u, *weights), state)

    def step_all(state, heat):
        return lax.map(lambda pair: advance(pair[0], pair[1], neighbours, send_rows, diffusion, transport), (state, heat))

    heat1 = heat_all(state0)
    state1 = step_all(state0, heat0)
    state2 = step_all(state1, heat1)
    heat2 = heat_all(state1)
    radiat2 = jnp.transpose(heat2.reshape(3, quarter, LEV, N_BLK * CELLS), (1, 0, 2, 3))
    return jnp.concatenate((radiat2.reshape(quarter, FIELDS, LEV, N_BLK * CELLS), state2), axis=0)
```

```python
import functools

import jax
import jax.numpy as jnp
from jax import lax
from jax.experimental import pallas as pl
from jax.experimental.pallas import tpu as pltpu
from jax.sharding import PartitionSpec as P

heat_gain = 0.5
bf16, f32 = jnp.bfloat16, jnp.float32


def dot(a, b):
    return jnp.dot(a, b, preferred_element_type=f32)


def pick_matrix(rows_ref, cells):
    halo = rows_ref.shape[1]
    cell = lax.broadcasted_iota(jnp.int32, (cells, halo), 0)
    return jnp.concatenate(
        [(cell == rows_ref[side : side + 1, :]).astype(bf16) for side in range(2)], axis=1
    )


def load_rows(ref, first, rows, cells):
    tiles = cells // 128
    return jnp.concatenate(
        [ref[pl.ds(first * tiles + tile, rows, stride=tiles), :] for tile in range(tiles)], axis=1
    )


def pack_kernel(held_ref, rows_ref, *out_refs):
    *slot_refs, state_ref, lower_ref, upper_ref = out_refs
    features, cells = state_ref.shape
    state = load_rows(held_ref, 0, features, cells).astype(bf16)
    state_ref[...] = state
    halo = rows_ref.shape[1]
    sent = dot(state, pick_matrix(rows_ref, cells)).astype(bf16)
    lower_ref[...] = sent[:, :halo]
    upper_ref[...] = sent[:, halo:]
    size = slot_refs[0].shape[0]
    for index, ref in enumerate(slot_refs):
        ref[...] = held_ref[index * size : (index + 1) * size, :]


def silu(v):
    half = 0.5 * v
    return half + half * jnp.tanh(half)


def network(state, w_in_ref, b_in_ref, w_mid_ref, b_mid_ref, w_out_ref, b_out_ref):
    def bias(ref):
        return jnp.concatenate([ref[...]] * (state.shape[1] // ref.shape[1]), axis=1)

    first = silu(dot(w_in_ref[...], state) + bias(b_in_ref)).astype(bf16)
    second = silu(dot(w_mid_ref[...], first) + bias(b_mid_ref)).astype(bf16)
    return dot(w_out_ref[...], second) + bias(b_out_ref)


def first_kernel(
    held_ref, state_ref, near_ref, diff_ref, tran_ref,
    w_in_t_ref, b_in_ref, w_mid_ref, b_mid_ref, w_out_ref, b_out_ref,
    heat_ref, matrix_ref, matrix_low_ref, keep_ref, part_ref, w_in_ref, c_in_ref, c_mid_ref, c_out_ref,
):
    features, cells = state_ref.shape
    w_in_ref[...] = w_in_t_ref[...].T
    for row_ref, column_ref in ((b_in_ref, c_in_ref), (b_mid_ref, c_mid_ref), (b_out_ref, c_out_ref)):
        column_ref[...] = jnp.broadcast_to(row_ref[...], (128, row_ref.shape[1])).T
    heat_ref[...] = network(
        state_ref[...], w_in_ref, c_in_ref, w_mid_ref, c_mid_ref, w_out_ref, c_out_ref
    )
    half_tran = 0.5 * tran_ref[...]
    weight = diff_ref[...] - half_tran
    keep = 1.0 - jnp.sum(diff_ref[...] + half_tran, axis=0, keepdims=True)
    keep_ref[...] = keep
    piece = 128
    for start in range(0, matrix_ref.shape[0], piece):
        cell = lax.broadcasted_iota(jnp.int32, (piece, cells), 0) + start
        total = jnp.zeros((piece, cells), f32)
        for edge in range(near_ref.shape[0]):
            total = total + jnp.where(
                cell == near_ref[edge : edge + 1, :], weight[edge : edge + 1, :], 0.0
            )
        high = total.astype(bf16)
        matrix_ref[start : start + piece, :] = high
        matrix_low_ref[start : start + piece, :] = (total - high.astype(f32)).astype(bf16)
    state = load_rows(held_ref, 0, features, cells)
    low = (state - state_ref[...].astype(f32)).astype(bf16)
    part_ref[...] = (
        dot(state_ref[...], matrix_ref[:cells, :])
        + dot(state_ref[...], matrix_low_ref[:cells, :])
        + dot(low, matrix_ref[:cells, :])
        + state * keep
    )


def halo_sum(matrix_ref, from_lower, from_upper):
    cells, halo = matrix_ref.shape[1], from_lower.shape[1]
    return dot(from_lower, matrix_ref[cells : cells + halo, :]) + dot(
        from_upper, matrix_ref[cells + halo :, :]
    )


def middle_kernel(
    slot_ref, rows_ref, part_ref, matrix_ref, matrix_low_ref, from_lower_ref, from_upper_ref, *refs
):
    *heat_refs, state_ref, state_bf_ref, lower_ref, upper_ref = refs
    cells, halo = matrix_ref.shape[1], rows_ref.shape[1]
    levels = heat_refs[0].shape[0] * 128 // cells
    slot = slot_ref[0]
    from_lower, from_upper = from_lower_ref[...], from_upper_ref[...]
    state_ref[...] = (
        part_ref[...]
        + halo_sum(matrix_ref, from_lower, from_upper)
        + halo_sum(matrix_low_ref, from_lower, from_upper)
    )
    for index, ref in enumerate(heat_refs):

        @pl.when(slot == index + 1)
        def _():
            state_ref[:levels, :] = state_ref[:levels, :] + heat_gain * load_rows(ref, 0, levels, cells)

    state = state_ref[...].astype(bf16)
    state_bf_ref[...] = state
    sent = dot(state, pick_matrix(rows_ref, cells)).astype(bf16)
    lower_ref[...] = sent[:, :halo]
    upper_ref[...] = sent[:, halo:]


def second_kernel(
    state_ref, w_in_ref, b_in_ref, w_mid_ref, b_mid_ref, w_out_ref, b_out_ref, heat_ref
):
    heat_ref[...] = network(
        state_ref[...], w_in_ref, b_in_ref, w_mid_ref, b_mid_ref, w_out_ref, b_out_ref
    ).astype(bf16)


def own_kernel(state_ref, state_bf_ref, matrix_ref, keep_ref, heat_ref, part_ref):
    cells, levels = matrix_ref.shape[1], heat_ref.shape[0]
    part_ref[...] = dot(state_bf_ref[...], matrix_ref[:cells, :]) + state_ref[...] * keep_ref[...]
    part_ref[:levels, :] = part_ref[:levels, :] + heat_gain * heat_ref[...]


def last_kernel(slot_ref, part_ref, matrix_ref, from_lower_ref, from_upper_ref, *refs):
    *heat_refs, out_ref = refs
    cells = matrix_ref.shape[1]
    tiles = cells // 128
    levels = heat_refs[0].shape[0]

    def store_rows(first, values):
        for tile in range(tiles):
            out_ref[pl.ds(first * tiles + tile, values.shape[0], stride=tiles), :] = values[
                :, tile * 128 : (tile + 1) * 128
            ]

    @pl.when(slot_ref[0] == 0)
    def _():
        for index, ref in enumerate(heat_refs):
            store_rows(index * levels, ref[...].astype(f32))

    @pl.when(slot_ref[0] != 0)
    def _():
        store_rows(
            0, part_ref[...] + halo_sum(matrix_ref, from_lower_ref[...], from_upper_ref[...])
        )


VMEM = pl.BlockSpec(memory_space=pltpu.VMEM)
SMEM = pl.BlockSpec(memory_space=pltpu.SMEM)


def call(kernel, name, out_shape, scalars, *args, flops=0, limit=16 << 20):
    size = sum(a.size * a.dtype.itemsize for a in args)
    return pl.pallas_call(
        kernel,
        out_shape=out_shape,
        in_specs=[SMEM] * scalars + [VMEM] * (len(args) - scalars),
        out_specs=jax.tree.map(lambda _: VMEM, out_shape),
        compiler_params=pltpu.CompilerParams(vmem_limit_bytes=limit),
        cost_estimate=pl.CostEstimate(flops=flops, bytes_accessed=size, transcendentals=0),
        name=name,
    )(*args)


def body(held, neighbours, send_rows, diffusion, transport, w_in, b_in, w_mid, b_mid, w_out, b_out):
    groups, blocks = lax.axis_size("grp"), lax.axis_size("blk")
    quarter = groups // 4
    slot = (lax.axis_index("grp") // quarter).astype(jnp.int32).reshape(1)
    _, fields, levels, cells = held.shape
    halo = send_rows.shape[1]
    hidden = w_mid.shape[0]
    features = fields * levels
    up = [(i, (i + 1) % blocks) for i in range(blocks)]
    down = [(j, i) for i, j in up]

    def swap(array, slot):
        to = {0: slot, slot: 0}
        pairs = [
            (g, to.get(g // quarter, g // quarter) * quarter + g % quarter) for g in range(groups)
        ]
        return lax.ppermute(array, "grp", pairs)

    def shape(*dims, dtype=f32):
        return jax.ShapeDtypeStruct(dims, dtype)

    halo_shape = shape(features, halo, dtype=bf16)
    state_shape = shape(features, cells, dtype=bf16)
    matrix_shape = shape(cells + 2 * halo, cells, dtype=bf16)
    flat = held.reshape(features * cells // 128, 128)
    *slots, state0, lower0, upper0 = call(
        pack_kernel, "pack",
        [shape(levels * cells // 128, 128)] * 3 + [state_shape, halo_shape, halo_shape],
        0, flat, send_rows, flops=2 * features * cells * 2 * halo,
    )
    from_lower0 = lax.ppermute(upper0, "blk", up)
    from_upper0 = lax.ppermute(lower0, "blk", down)
    heats0 = [swap(array, index + 1) for index, array in enumerate(slots)]
    heat1, matrix, matrix_low, keep, part1, *weights = call(
        first_kernel, "first",
        [
            shape(levels, cells), matrix_shape, matrix_shape, shape(1, cells), shape(features, cells),
            shape(hidden, features, dtype=bf16), shape(hidden, 128), shape(hidden, 128), shape(levels, 128),
        ],
        0, flat, state0, neighbours, diffusion, transport,
        w_in.T, b_in[None], w_mid, b_mid[None], w_out, b_out[None],
        flops=2 * cells * hidden * (hidden + features),
    )
    w_in_n, c_in, c_mid, c_out = weights
    state1, state1_bf, lower1, upper1 = call(
        middle_kernel, "middle",
        [shape(features, cells), state_shape, halo_shape, halo_shape],
        1, slot, send_rows, part1, matrix, matrix_low, from_lower0, from_upper0, *heats0,
        flops=2 * features * cells * 2 * halo,
    )
    from_lower1 = lax.ppermute(upper1, "blk", up)
    from_upper1 = lax.ppermute(lower1, "blk", down)
    heat2 = call(
        second_kernel, "second", shape(levels, cells, dtype=bf16),
        0, state1_bf, w_in_n, c_in, w_mid, c_mid, w_out, c_out,
        flops=2 * cells * hidden * (hidden + features),
    )
    heats2 = [swap(heat2, index + 1) for index in range(3)]
    part2 = call(
        own_kernel, "own", shape(features, cells),
        0, state1, state1_bf, matrix, keep, heat1, flops=2 * features * cells * cells,
    )
    out = call(
        last_kernel, "last", shape(*flat.shape),
        1, slot, part2, matrix, from_lower1, from_upper1, *heats2, flops=2 * features * cells * 2 * halo,
    )
    return out.reshape(held.shape)


def solution(mesh):
    placed = (
        P("grp", None, None, "blk"),
        P(None, "blk"),
        P(None, "blk"),
        P(None, "blk"),
        P(None, "blk"),
        P(),
        P(),
        P(),
        P(),
        P(),
        P(),
    )
    return jax.shard_map(
        body, mesh=mesh, in_specs=placed, out_specs=P("grp", None, None, "blk"), check_vma=False
    )
```

```python
import math

import jax
import jax.numpy as jnp
from jax import lax
from jax.experimental import pallas as pl
from jax.experimental.pallas import tpu as pltpu
from jax.sharding import PartitionSpec as P

heat_gain = 0.5
bf16, f32, i16 = jnp.bfloat16, jnp.float32, jnp.int16

plan0 = ("HBA", "BHA", "BAH")
plan1 = ("HBA", "BHA", "BAH")


def dot(a, b):
    return jnp.dot(a, b, preferred_element_type=f32)


def split(values):
    high = values.astype(bf16)
    return high, (values - high.astype(f32)).astype(bf16)


def position(quarter):
    return lax.axis_index("grp") // quarter, lax.axis_index("blk") % 2


def load_rows(ref, first, rows, cells):
    tiles = cells // 128
    return jnp.concatenate(
        [ref[pl.ds(first * tiles + tile, rows, stride=tiles), :] for tile in range(tiles)], axis=1
    )


def encode(values):
    largest = jnp.max(jnp.max(jnp.abs(values), axis=0, keepdims=True), axis=1, keepdims=True)
    power = jnp.ceil(jnp.log(jnp.maximum(largest, 1e-30) * (1 / 32000)) * (1 / math.log(2)))
    return jnp.round(values * jnp.exp2(-power)), jnp.broadcast_to(power, (16, 128))


def put(message_ref, codes, power, stride):
    for tile in range(codes.shape[1] // 128):
        message_ref[tile * stride : (tile + 1) * stride, :] = (
            codes[:, tile * 128 : (tile + 1) * 128].astype(jnp.int32).astype(i16)
        )
    message_ref[-16:, :] = power.astype(jnp.int32).astype(i16)


def take(message_ref, stride, tiles):
    scale = jnp.exp2(message_ref[-16:, :].astype(f32)[:1])
    return jnp.concatenate(
        [
            message_ref[tile * stride : (tile + 1) * stride, :].astype(f32) * scale
            for tile in range(tiles)
        ],
        axis=1,
    )


def put_halos(plan, slot, odd, message_refs, codes, power):
    halo = codes.shape[1] // 2
    lower, upper = codes[:, :halo], codes[:, halo:]
    pair = {"A": jnp.where(odd == 0, upper, lower), "B": jnp.where(odd == 0, lower, upper)}
    for group, kinds in enumerate(plan):

        @pl.when(slot == group + 1)
        def _():
            for kind, ref in zip(kinds, message_refs):
                if kind != "H":
                    put(ref, pair[kind], power, codes.shape[0])


def take_halos(plan, slot, odd, message_refs, halo_ref):
    rows = halo_ref.shape[1]
    for group, kinds in enumerate(plan):

        @pl.when(slot == group + 1)
        def _():
            for kind, ref in zip(kinds, message_refs):
                if kind != "H":
                    side = 1 - odd if kind == "A" else odd
                    halo_ref[side] = take(ref, rows, 1)


def pack_kernel(quarter, features, *refs):
    count = (len(refs) - 9) // 2
    held_hbm, rows_hbm, *others_hbm = refs[: count + 2]
    first_ref, second_ref, third_ref, held_ref, rows_ref = refs[count + 2 : count + 7]
    others, (pick_ref, sems) = refs[count + 7 : -2], refs[-2:]
    messages = (first_ref, second_ref, third_ref)
    copies = [
        pltpu.make_async_copy(held_hbm, held_ref.at[pl.ds(0, held_hbm.shape[0])], sems.at[0]),
        pltpu.make_async_copy(rows_hbm, rows_ref, sems.at[1]),
    ]
    for index, (source, target) in enumerate(zip(others_hbm, others)):
        copies.append(pltpu.make_async_copy(source, target, sems.at[index + 2]))
    for copy in copies:
        copy.start()
    slot, odd = position(quarter)
    cells = pick_ref.shape[0]
    rows, halo = held_ref.shape[0] * 128 // cells, rows_ref.shape[1]
    held_ref[held_hbm.shape[0] :, :] = jnp.zeros(
        (held_ref.shape[0] - held_hbm.shape[0], 128), f32
    )
    copies[1].wait()
    cell = lax.broadcasted_iota(jnp.int32, (cells, halo), 0)
    for side in range(2):
        pick_ref[:, side * halo : (side + 1) * halo] = (
            cell == rows_ref[side : side + 1, :]
        ).astype(bf16)
    copies[0].wait()
    levels = features // 3

    @pl.when(slot == 0)
    def _():
        stride = -(-levels // 16) * 16
        for group, kinds in enumerate(plan0):
            codes, power = encode(load_rows(held_ref, group * levels, levels, cells))
            codes = jnp.concatenate([codes, jnp.zeros((stride - levels, cells), f32)], axis=0)
            put(messages[kinds.index("H")], codes, power, stride)

    @pl.when(slot != 0)
    def _():
        high, low = split(load_rows(held_ref, 0, rows, cells))
        codes, power = encode(dot(high, pick_ref[...]) + dot(low, pick_ref[...]))
        put_halos(plan0, slot, odd, messages, codes, power)

    for copy in copies[2:]:
        copy.wait()


def silu(v):
    half = 0.5 * v
    return half + half * jnp.tanh(half)


def network(state, w_in_ref, b_in_ref, w_mid_ref, b_mid_ref, w_out_ref, b_out_ref):
    def bias(ref):
        return jnp.concatenate([ref[...]] * (state.shape[1] // ref.shape[1]), axis=1)

    first = silu(dot(w_in_ref[...], state) + bias(b_in_ref)).astype(bf16)
    second = silu(dot(w_mid_ref[...], first) + bias(b_mid_ref)).astype(bf16)
    return dot(w_out_ref[...], second) + bias(b_out_ref)


def first_kernel(
    held_ref, near_ref, diff_ref, tran_ref, w_in_t_ref, b_in_ref, b_mid_ref, b_out_ref,
    matrix_ref, matrix_low_ref, keep_ref, part_ref, w_in_ref, c_in_ref, c_mid_ref, c_out_ref,
):
    rows, cells = part_ref.shape
    half_tran = 0.5 * tran_ref[...]
    weight = diff_ref[...] - half_tran
    keep = 1.0 - jnp.sum(diff_ref[...] + half_tran, axis=0, keepdims=True)
    keep_ref[...] = keep
    piece = 128
    for start in range(0, matrix_ref.shape[0], piece):
        cell = lax.broadcasted_iota(jnp.int32, (piece, cells), 0) + start
        total = jnp.zeros((piece, cells), f32)
        for edge in range(near_ref.shape[0]):
            total = total + jnp.where(
                cell == near_ref[edge : edge + 1, :], weight[edge : edge + 1, :], 0.0
            )
        matrix_ref[start : start + piece, :], matrix_low_ref[start : start + piece, :] = split(total)
    state = load_rows(held_ref, 0, rows, cells)
    high, low = split(state)
    part_ref[...] = (
        dot(high, matrix_ref[:cells, :])
        + dot(high, matrix_low_ref[:cells, :])
        + dot(low, matrix_ref[:cells, :])
        + state * keep
    )
    features = w_in_t_ref.shape[0]
    w_in_ref[...] = jnp.zeros_like(w_in_ref)
    w_in_ref[:, :features] = w_in_t_ref[...].T
    for row_ref, column_ref in ((b_in_ref, c_in_ref), (b_mid_ref, c_mid_ref), (b_out_ref, c_out_ref)):
        column_ref[...] = jnp.broadcast_to(row_ref[...], (128, row_ref.shape[1])).T


def middle_kernel(
    quarter, first_in, second_in, third_in, pick_ref, part_ref, matrix_ref, matrix_low_ref,
    w_in_ref, b_in_ref, w_mid_ref, b_mid_ref, w_out_ref, b_out_ref,
    first_out, second_out, third_out, state_ref, halo_ref,
):
    slot, odd = position(quarter)
    received, messages = (first_in, second_in, third_in), (first_out, second_out, third_out)
    cells, halo = matrix_ref.shape[1], halo_ref.shape[2]
    levels = w_out_ref.shape[0]
    stride = -(-levels // 16) * 16
    take_halos(plan0, slot, odd, received, halo_ref)
    total = part_ref[...]
    for side in range(2):
        high, low = split(halo_ref[side])
        place = slice(cells + side * halo, cells + (side + 1) * halo)
        total = (
            total
            + dot(high, matrix_ref[place, :])
            + dot(high, matrix_low_ref[place, :])
            + dot(low, matrix_ref[place, :])
        )
    state_ref[...] = total
    for group, kinds in enumerate(plan0):

        @pl.when(slot == group + 1)
        def _():
            heat = take(received[kinds.index("H")], stride, cells // 128)[:levels]
            state_ref[:levels, :] = state_ref[:levels, :] + heat_gain * heat

    state = state_ref[...].astype(bf16)
    codes, power = encode(dot(state, pick_ref[...]))
    put_halos(plan1, slot, odd, messages, codes, power)
    codes, power = encode(
        network(state, w_in_ref, b_in_ref, w_mid_ref, b_mid_ref, w_out_ref, b_out_ref)
    )
    codes = jnp.concatenate([codes, jnp.zeros((stride - levels, cells), f32)], axis=0)
    for group, kinds in enumerate(plan1):

        @pl.when(slot == group + 1)
        def _():
            put(messages[kinds.index("H")], codes, power, stride)


def own_kernel(
    held_ref, state_ref, matrix_ref, keep_ref,
    w_in_ref, b_in_ref, w_mid_ref, b_mid_ref, w_out_ref, b_out_ref, part_ref,
):
    rows, cells = state_ref.shape
    levels = w_out_ref.shape[0]
    start = load_rows(held_ref, 0, rows, cells).astype(bf16)
    heat = network(start, w_in_ref, b_in_ref, w_mid_ref, b_mid_ref, w_out_ref, b_out_ref)
    state = state_ref[...]
    part_ref[...] = dot(state.astype(bf16), matrix_ref[:cells, :]) + state * keep_ref[...]
    part_ref[:levels, :] = part_ref[:levels, :] + heat_gain * heat


def last_kernel(
    quarter, first_in, second_in, third_in, part_ref, matrix_ref, out_ref, halo_ref
):
    slot, odd = position(quarter)
    received = (first_in, second_in, third_in)
    cells, halo = matrix_ref.shape[1], halo_ref.shape[2]
    tiles = cells // 128
    features = out_ref.shape[0] // tiles
    levels = features // 3
    stride = -(-levels // 16) * 16

    def store_rows(first, values):
        for tile in range(tiles):
            out_ref[pl.ds(first * tiles + tile, values.shape[0], stride=tiles), :] = values[
                :, tile * 128 : (tile + 1) * 128
            ]

    @pl.when(slot == 0)
    def _():
        for group, kinds in enumerate(plan1):
            store_rows(group * levels, take(received[kinds.index("H")], stride, tiles)[:levels])

    take_halos(plan1, slot, odd, received, halo_ref)

    @pl.when(slot != 0)
    def _():
        total = part_ref[...]
        for side in range(2):
            place = slice(cells + side * halo, cells + (side + 1) * halo)
            total = total + dot(halo_ref[side].astype(bf16), matrix_ref[place, :])
        store_rows(0, total[:features])


VMEM = pl.BlockSpec(memory_space=pltpu.VMEM)
HBM = pl.BlockSpec(memory_space=pltpu.HBM)


def call(kernel, name, out_shape, *args, place=VMEM, scratch=(), flops=0, limit=16 << 20):
    size = sum(a.size * a.dtype.itemsize for a in args)
    if place is HBM:
        args = [pltpu.with_memory_space_constraint(a, pltpu.HBM) for a in args]
    return pl.pallas_call(
        kernel,
        out_shape=out_shape,
        in_specs=[place] * len(args),
        out_specs=jax.tree.map(lambda _: VMEM, out_shape),
        scratch_shapes=scratch,
        compiler_params=pltpu.CompilerParams(vmem_limit_bytes=limit),
        cost_estimate=pl.CostEstimate(flops=flops, bytes_accessed=size, transcendentals=0),
        name=name,
    )(*args)


def exchange(plan, messages, quarter, blocks):
    def partner(group, block, step):
        slot, place = group // quarter, group % quarter
        kinds = [kinds[step] for kinds in plan]
        if slot == 0:
            return (kinds.index("H") + 1) * quarter + place, block
        kind = kinds[slot - 1]
        if kind == "H":
            return place, block
        up = (block % 2 == 0) == (kind == "A")
        return group, (block + (1 if up else -1)) % blocks

    received = []
    for step, message in enumerate(messages):
        pairs = []
        for group in range(4 * quarter):
            for block in range(blocks):
                to_group, to_block = partner(group, block, step)
                pairs.append((group * blocks + block, to_group * blocks + to_block))
        received.append(lax.ppermute(message, ("grp", "blk"), pairs))
    return received


def body(held, neighbours, send_rows, diffusion, transport, w_in, b_in, w_mid, b_mid, w_out, b_out):
    quarter, blocks = lax.axis_size("grp") // 4, lax.axis_size("blk")
    _, fields, levels, cells = held.shape
    halo, hidden = send_rows.shape[1], w_mid.shape[0]
    features, tiles = fields * levels, cells // 128
    rows = -(-features // 16) * 16
    length = max(-(-levels // 16) * 16 * tiles, rows) + 16

    def shape(*dims, dtype=f32):
        return jax.ShapeDtypeStruct(dims, dtype)

    def like(array):
        return shape(*array.shape, dtype=array.dtype)

    message = shape(length, 128, dtype=i16)
    full = shape(rows, cells)
    matrix_shape = shape(cells + 2 * halo, cells, dtype=bf16)
    halos = pltpu.VMEM((2, rows, halo), f32)
    args = (neighbours, diffusion, transport, w_in.T, b_in[None], b_mid[None], b_out[None], w_mid, w_out)
    *messages, flat, _, near, diff, tran, w_in_t, b_in, b_mid, b_out, w_mid, w_out, pick = call(
        lambda *refs: pack_kernel(quarter, features, *refs), "pack",
        [message] * 3
        + [shape(rows * tiles, 128), like(send_rows)]
        + [like(array) for array in args]
        + [shape(cells, 2 * halo, dtype=bf16)],
        held.reshape(features * tiles, 128), send_rows, *args,
        place=HBM, scratch=[pltpu.SemaphoreType.DMA((2 + len(args),))],
    )
    received = exchange(plan0, messages, quarter, blocks)
    matrix, matrix_low, keep, part1, w_in, c_in, c_mid, c_out = call(
        first_kernel, "first",
        [
            matrix_shape, matrix_shape, shape(1, cells), full,
            shape(hidden, rows, dtype=bf16), shape(hidden, 128), shape(hidden, 128), shape(levels, 128),
        ],
        flat, near, diff, tran, w_in_t, b_in, b_mid, b_out, flops=2 * cells * hidden * hidden,
    )
    weights = (w_in, c_in, w_mid, c_mid, w_out, c_out)
    *messages, state1 = call(
        lambda *refs: middle_kernel(quarter, *refs), "middle",
        [message] * 3 + [full],
        *received, pick, part1, matrix, matrix_low, *weights,
        scratch=[halos], flops=2 * cells * hidden * hidden,
    )
    received = exchange(plan1, messages, quarter, blocks)
    part2 = call(
        own_kernel, "own", full, flat, state1, matrix, keep, *weights, flops=2 * cells * hidden * hidden
    )
    out = call(
        lambda *refs: last_kernel(quarter, *refs), "last", shape(features * tiles, 128),
        *received, part2, matrix, scratch=[halos], flops=2 * rows * cells * 2 * halo,
    )
    return out.reshape(held.shape)


def solution(mesh):
    placed = (
        P("grp", None, None, "blk"),
        P(None, "blk"),
        P(None, "blk"),
        P(None, "blk"),
        P(None, "blk"),
        P(),
        P(),
        P(),
        P(),
        P(),
        P(),
    )
    return jax.shard_map(
        body, mesh=mesh, in_specs=placed, out_specs=P("grp", None, None, "blk"), check_vma=False
    )
```

```python
import math

import jax
import jax.numpy as jnp
from jax import lax
from jax.experimental import pallas as pl
from jax.experimental.pallas import tpu as pltpu
from jax.sharding import PartitionSpec as P

heat_gain = 0.5
bf16, f32, i16 = jnp.bfloat16, jnp.float32, jnp.int16

plan0 = ("HAB", "AHB", "ABH")
plan1 = ("HAB", "AHB", "ABH")


def dot(a, b):
    return jnp.dot(a, b, preferred_element_type=f32)


def split(values):
    high = values.astype(bf16)
    return high, (values - high.astype(f32)).astype(bf16)


def position(quarter):
    return lax.axis_index("grp") // quarter, lax.axis_index("blk") % 2


def load_rows(ref, first, rows, cells):
    tiles = cells // 128
    return jnp.concatenate(
        [ref[pl.ds(first * tiles + tile, rows, stride=tiles), :] for tile in range(tiles)], axis=1
    )


def encode(values):
    largest = jnp.max(jnp.max(jnp.abs(values), axis=0, keepdims=True), axis=1, keepdims=True)
    power = jnp.ceil(jnp.log(jnp.maximum(largest, 1e-30) * (1 / 32000)) * (1 / math.log(2)))
    return jnp.round(values * jnp.exp2(-power)), jnp.broadcast_to(power, (16, 128))


def put(message_ref, codes, power, stride):
    for tile in range(codes.shape[1] // 128):
        message_ref[tile * stride : (tile + 1) * stride, :] = (
            codes[:, tile * 128 : (tile + 1) * 128].astype(jnp.int32).astype(i16)
        )
    message_ref[-16:, :] = power.astype(jnp.int32).astype(i16)


def take(message_ref, stride, tiles):
    scale = jnp.exp2(message_ref[-16:, :].astype(f32)[:1])
    return jnp.concatenate(
        [
            message_ref[tile * stride : (tile + 1) * stride, :].astype(f32) * scale
            for tile in range(tiles)
        ],
        axis=1,
    )


def put_halos(plan, slot, odd, message_refs, codes, power):
    halo = codes.shape[1] // 2
    lower, upper = codes[:, :halo], codes[:, halo:]
    pair = {"A": jnp.where(odd == 0, upper, lower), "B": jnp.where(odd == 0, lower, upper)}
    for group, kinds in enumerate(plan):

        @pl.when(slot == group + 1)
        def _():
            for kind, ref in zip(kinds, message_refs):
                if kind in pair:
                    put(ref, pair[kind], power, codes.shape[0])


def take_halos(plan, slot, odd, message_refs, halo_ref):
    rows = halo_ref.shape[1]
    for group, kinds in enumerate(plan):

        @pl.when(slot == group + 1)
        def _():
            for kind, ref in zip(kinds, message_refs):
                if kind in ("A", "B"):
                    side = 1 - odd if kind == "A" else odd
                    halo_ref[side] = take(ref, rows, 1)


def pack_kernel(quarter, features, *refs):
    steps = len(plan0[0])
    count = (len(refs) - steps - 6) // 2
    held_hbm, rows_hbm, *others_hbm = refs[: count + 2]
    *messages, held_ref, rows_ref = refs[count + 2 : count + steps + 4]
    others, (pick_ref, sems) = refs[count + steps + 4 : -2], refs[-2:]
    copies = [
        pltpu.make_async_copy(held_hbm, held_ref.at[pl.ds(0, held_hbm.shape[0])], sems.at[0]),
        pltpu.make_async_copy(rows_hbm, rows_ref, sems.at[1]),
    ]
    for index, (source, target) in enumerate(zip(others_hbm, others)):
        copies.append(pltpu.make_async_copy(source, target, sems.at[index + 2]))
    for copy in copies:
        copy.start()
    slot, odd = position(quarter)
    cells = pick_ref.shape[0]
    rows, halo = held_ref.shape[0] * 128 // cells, rows_ref.shape[1]
    held_ref[held_hbm.shape[0] :, :] = jnp.zeros(
        (held_ref.shape[0] - held_hbm.shape[0], 128), f32
    )
    copies[1].wait()
    cell = lax.broadcasted_iota(jnp.int32, (cells, halo), 0)
    for side in range(2):
        pick_ref[:, side * halo : (side + 1) * halo] = (
            cell == rows_ref[side : side + 1, :]
        ).astype(bf16)
    copies[0].wait()
    levels = features // 3

    @pl.when(slot == 0)
    def _():
        stride = -(-levels // 16) * 16
        for group, kinds in enumerate(plan0):
            codes, power = encode(load_rows(held_ref, group * levels, levels, cells))
            codes = jnp.concatenate([codes, jnp.zeros((stride - levels, cells), f32)], axis=0)
            put(messages[kinds.index("H")], codes, power, stride)

    @pl.when(slot != 0)
    def _():
        high, low = split(load_rows(held_ref, 0, rows, cells))
        codes, power = encode(dot(high, pick_ref[...]) + dot(low, pick_ref[...]))
        put_halos(plan0, slot, odd, messages, codes, power)

    for copy in copies[2:]:
        copy.wait()


def silu(v):
    half = 0.5 * v
    return half + half * jnp.tanh(half)


def network(state, w_in_ref, b_in_ref, w_mid_ref, b_mid_ref, w_out_ref, b_out_ref):
    def bias(ref):
        return jnp.concatenate([ref[...]] * (state.shape[1] // ref.shape[1]), axis=1)

    first = silu(dot(w_in_ref[...], state) + bias(b_in_ref)).astype(bf16)
    second = silu(dot(w_mid_ref[...], first) + bias(b_mid_ref)).astype(bf16)
    return dot(w_out_ref[...], second) + bias(b_out_ref)


def first_kernel(
    held_ref, near_ref, diff_ref, tran_ref, w_in_t_ref, b_in_ref, b_mid_ref, b_out_ref,
    matrix_ref, matrix_low_ref, keep_ref, part_ref, w_in_ref, c_in_ref, c_mid_ref, c_out_ref,
):
    rows, cells = part_ref.shape
    half_tran = 0.5 * tran_ref[...]
    weight = diff_ref[...] - half_tran
    keep = 1.0 - jnp.sum(diff_ref[...] + half_tran, axis=0, keepdims=True)
    keep_ref[...] = keep
    piece = 128
    for start in range(0, matrix_ref.shape[0], piece):
        cell = lax.broadcasted_iota(jnp.int32, (piece, cells), 0) + start
        total = jnp.zeros((piece, cells), f32)
        for edge in range(near_ref.shape[0]):
            total = total + jnp.where(
                cell == near_ref[edge : edge + 1, :], weight[edge : edge + 1, :], 0.0
            )
        matrix_ref[start : start + piece, :], matrix_low_ref[start : start + piece, :] = split(total)
    state = load_rows(held_ref, 0, rows, cells)
    high, low = split(state)
    part_ref[...] = (
        dot(high, matrix_ref[:cells, :])
        + dot(high, matrix_low_ref[:cells, :])
        + dot(low, matrix_ref[:cells, :])
        + state * keep
    )
    features = w_in_t_ref.shape[0]
    w_in_ref[...] = jnp.zeros_like(w_in_ref)
    w_in_ref[:, :features] = w_in_t_ref[...].T
    for row_ref, column_ref in ((b_in_ref, c_in_ref), (b_mid_ref, c_mid_ref), (b_out_ref, c_out_ref)):
        column_ref[...] = jnp.broadcast_to(row_ref[...], (128, row_ref.shape[1])).T


def middle_kernel(
    quarter, received, pick_ref, part_ref, matrix_ref, matrix_low_ref,
    w_in_ref, b_in_ref, w_mid_ref, b_mid_ref, w_out_ref, b_out_ref,
    messages, state_ref, halo_ref,
):
    slot, odd = position(quarter)
    cells, halo = matrix_ref.shape[1], halo_ref.shape[2]
    levels = w_out_ref.shape[0]
    stride = -(-levels // 16) * 16
    take_halos(plan0, slot, odd, received, halo_ref)
    total = part_ref[...]
    for side in range(2):
        high, low = split(halo_ref[side])
        place = slice(cells + side * halo, cells + (side + 1) * halo)
        total = (
            total
            + dot(high, matrix_ref[place, :])
            + dot(high, matrix_low_ref[place, :])
            + dot(low, matrix_ref[place, :])
        )
    state_ref[...] = total
    for group, kinds in enumerate(plan0):

        @pl.when(slot == group + 1)
        def _():
            heat = take(received[kinds.index("H")], stride, cells // 128)[:levels]
            state_ref[:levels, :] = state_ref[:levels, :] + heat_gain * heat

    state = state_ref[...].astype(bf16)
    codes, power = encode(dot(state, pick_ref[...]))
    put_halos(plan1, slot, odd, messages, codes, power)
    codes, power = encode(
        network(state, w_in_ref, b_in_ref, w_mid_ref, b_mid_ref, w_out_ref, b_out_ref)
    )
    codes = jnp.concatenate([codes, jnp.zeros((stride - levels, cells), f32)], axis=0)
    for group, kinds in enumerate(plan1):

        @pl.when(slot == group + 1)
        def _():
            put(messages[kinds.index("H")], codes, power, stride)


def own_kernel(
    held_ref, state_ref, matrix_ref, keep_ref,
    w_in_ref, b_in_ref, w_mid_ref, b_mid_ref, w_out_ref, b_out_ref, part_ref,
):
    rows, cells = state_ref.shape
    levels = w_out_ref.shape[0]
    start = load_rows(held_ref, 0, rows, cells).astype(bf16)
    heat = network(start, w_in_ref, b_in_ref, w_mid_ref, b_mid_ref, w_out_ref, b_out_ref)
    state = state_ref[...]
    part_ref[...] = dot(state.astype(bf16), matrix_ref[:cells, :]) + state * keep_ref[...]
    part_ref[:levels, :] = part_ref[:levels, :] + heat_gain * heat


def last_kernel(quarter, received, part_ref, matrix_ref, out_ref, halo_ref):
    slot, odd = position(quarter)
    cells, halo = matrix_ref.shape[1], halo_ref.shape[2]
    tiles = cells // 128
    features = out_ref.shape[0] // tiles
    levels = features // 3
    stride = -(-levels // 16) * 16

    def store_rows(first, values):
        for tile in range(tiles):
            out_ref[pl.ds(first * tiles + tile, values.shape[0], stride=tiles), :] = values[
                :, tile * 128 : (tile + 1) * 128
            ]

    @pl.when(slot == 0)
    def _():
        for group, kinds in enumerate(plan1):
            store_rows(group * levels, take(received[kinds.index("H")], stride, tiles)[:levels])

    take_halos(plan1, slot, odd, received, halo_ref)

    @pl.when(slot != 0)
    def _():
        total = part_ref[...]
        for side in range(2):
            place = slice(cells + side * halo, cells + (side + 1) * halo)
            total = total + dot(halo_ref[side].astype(bf16), matrix_ref[place, :])
        store_rows(0, total[:features])


VMEM = pl.BlockSpec(memory_space=pltpu.VMEM)
HBM = pl.BlockSpec(memory_space=pltpu.HBM)


def call(kernel, name, out_shape, *args, place=VMEM, scratch=(), flops=0, limit=16 << 20):
    size = sum(a.size * a.dtype.itemsize for a in args)
    if place is HBM:
        args = [pltpu.with_memory_space_constraint(a, pltpu.HBM) for a in args]
    return pl.pallas_call(
        kernel,
        out_shape=out_shape,
        in_specs=[place] * len(args),
        out_specs=jax.tree.map(lambda _: VMEM, out_shape),
        scratch_shapes=scratch,
        compiler_params=pltpu.CompilerParams(vmem_limit_bytes=limit),
        cost_estimate=pl.CostEstimate(flops=flops, bytes_accessed=size, transcendentals=0),
        name=name,
    )(*args)


def exchange(plan, messages, quarter, blocks):
    def partner(group, block, step):
        slot, place = group // quarter, group % quarter
        kinds = [kinds[step] for kinds in plan]
        if slot == 0 and "H" in kinds:
            return (kinds.index("H") + 1) * quarter + place, block
        kind = kinds[slot - 1] if slot else "a"
        if kind == "H":
            return place, block
        up = (block % 2 == 0) == (kind != "B")
        return group, (block + (1 if up else -1)) % blocks

    received = []
    for step, message in enumerate(messages):
        pairs = []
        for group in range(4 * quarter):
            for block in range(blocks):
                to_group, to_block = partner(group, block, step)
                pairs.append((group * blocks + block, to_group * blocks + to_block))
        received.append(lax.ppermute(message, ("grp", "blk"), pairs))
    return received


def body(held, neighbours, send_rows, diffusion, transport, w_in, b_in, w_mid, b_mid, w_out, b_out):
    quarter, blocks = lax.axis_size("grp") // 4, lax.axis_size("blk")
    _, fields, levels, cells = held.shape
    halo, hidden = send_rows.shape[1], w_mid.shape[0]
    features, tiles = fields * levels, cells // 128
    rows = -(-features // 16) * 16
    length = max(-(-levels // 16) * 16 * tiles, rows) + 16

    def shape(*dims, dtype=f32):
        return jax.ShapeDtypeStruct(dims, dtype)

    def like(array):
        return shape(*array.shape, dtype=array.dtype)

    message = shape(length, 128, dtype=i16)
    full = shape(rows, cells)
    matrix_shape = shape(cells + 2 * halo, cells, dtype=bf16)
    halos = pltpu.VMEM((2, rows, halo), f32)
    count0, count1 = len(plan0[0]), len(plan1[0])
    args = (neighbours, diffusion, transport, w_in.T, b_in[None], b_mid[None], b_out[None], w_mid, w_out)
    *messages, flat, _, near, diff, tran, w_in_t, b_in, b_mid, b_out, w_mid, w_out, pick = call(
        lambda *refs: pack_kernel(quarter, features, *refs), "pack",
        [message] * len(plan0[0])
        + [shape(rows * tiles, 128), like(send_rows)]
        + [like(array) for array in args]
        + [shape(cells, 2 * halo, dtype=bf16)],
        held.reshape(features * tiles, 128), send_rows, *args,
        place=HBM, scratch=[pltpu.SemaphoreType.DMA((2 + len(args),))],
    )
    received = exchange(plan0, messages, quarter, blocks)
    matrix, matrix_low, keep, part1, w_in, c_in, c_mid, c_out = call(
        first_kernel, "first",
        [
            matrix_shape, matrix_shape, shape(1, cells), full,
            shape(hidden, rows, dtype=bf16), shape(hidden, 128), shape(hidden, 128), shape(levels, 128),
        ],
        flat, near, diff, tran, w_in_t, b_in, b_mid, b_out, flops=2 * cells * hidden * hidden,
    )
    weights = (w_in, c_in, w_mid, c_mid, w_out, c_out)
    *messages, state1 = call(
        lambda *refs: middle_kernel(
            quarter, refs[:count0], *refs[count0 : count0 + 10],
            refs[count0 + 10 : count0 + 10 + count1], *refs[count0 + 10 + count1 :],
        ),
        "middle", [message] * count1 + [full],
        *received, pick, part1, matrix, matrix_low, *weights,
        scratch=[halos], flops=2 * cells * hidden * hidden,
    )
    received = exchange(plan1, messages, quarter, blocks)
    part2 = call(
        own_kernel, "own", full, flat, state1, matrix, keep, *weights, flops=2 * cells * hidden * hidden
    )
    out = call(
        lambda *refs: last_kernel(quarter, refs[:count1], *refs[count1:]), "last", shape(features * tiles, 128),
        *received, part2, matrix, scratch=[halos], flops=2 * rows * cells * 2 * halo,
    )
    return out.reshape(held.shape)


def solution(mesh):
    placed = (
        P("grp", None, None, "blk"),
        P(None, "blk"),
        P(None, "blk"),
        P(None, "blk"),
        P(None, "blk"),
        P(),
        P(),
        P(),
        P(),
        P(),
        P(),
    )
    return jax.shard_map(
        body, mesh=mesh, in_specs=placed, out_specs=P("grp", None, None, "blk"), check_vma=False
    )
```

```python
import math

import jax
import jax.numpy as jnp
from jax import lax
from jax.experimental import pallas as pl
from jax.experimental.pallas import tpu as pltpu
from jax.sharding import PartitionSpec as P

heat_gain = 0.5
bf16, f32, i16 = jnp.bfloat16, jnp.float32, jnp.int16

plan0 = ("HAB", "AHB", "ABH")
plan1 = ("HAB", "AHB", "ABH")


def dot(a, b):
    return jnp.dot(a, b, preferred_element_type=f32)


def split(values):
    high = values.astype(bf16)
    return high, (values - high.astype(f32)).astype(bf16)


def position(quarter):
    return lax.axis_index("grp") // quarter, lax.axis_index("blk") % 2


def load_rows(ref, first, rows, cells):
    tiles = cells // 128
    return jnp.concatenate(
        [ref[pl.ds(first * tiles + tile, rows, stride=tiles), :] for tile in range(tiles)], axis=1
    )


def power_of(values):
    largest = jnp.max(jnp.max(jnp.abs(values), axis=0, keepdims=True), axis=1, keepdims=True)
    power = jnp.ceil(jnp.log(jnp.maximum(largest, 1e-30) * (1 / 32000)) * (1 / math.log(2)))
    return jnp.broadcast_to(power, (16, 128))


def padded(values, rows):
    spare = rows - values.shape[0]
    return jnp.concatenate([values, jnp.zeros((spare, values.shape[1]), f32)], axis=0) if spare else values


def to_message(codes, power, length):
    tiles = [codes[:, at : at + 128] for at in range(0, codes.shape[1], 128)]
    spare = length - 16 - len(tiles) * codes.shape[0]
    if spare:
        tiles.append(jnp.zeros((spare, 128), f32))
    return jnp.concatenate([*tiles, power], axis=0).astype(jnp.int32).astype(i16)


def from_message(message, rows, tiles):
    values = message.astype(f32)
    values = values[:-16] * jnp.exp2(values[-16:-15])
    return jnp.concatenate([values[at * rows : (at + 1) * rows] for at in range(tiles)], axis=1)


def halo_messages(odd, codes, power, length):
    halo = codes.shape[1] // 2
    lower, upper = (to_message(part, power, length) for part in (codes[:, :halo], codes[:, halo:]))
    return {"A": jnp.where(odd == 0, upper, lower), "B": jnp.where(odd == 0, lower, upper)}


def send(plan, slot, message_refs, messages):
    for step, ref in enumerate(message_refs):
        value = messages[plan[0][step]]
        for group in range(1, len(plan)):
            value = jnp.where(slot == group + 1, messages[plan[group][step]], value)
        ref[...] = value


def receive(plan, slot, message_refs, kind):
    value = message_refs[plan[0].index(kind)][...]
    for group in range(1, len(plan)):
        value = jnp.where(slot == group + 1, message_refs[plan[group].index(kind)][...], value)
    return value


def receive_halos(plan, slot, odd, message_refs, rows):
    near = from_message(receive(plan, slot, message_refs, "A"), rows, 1)
    far = from_message(receive(plan, slot, message_refs, "B"), rows, 1)
    return jnp.concatenate(
        [jnp.where(odd == 0, far, near), jnp.where(odd == 0, near, far)], axis=1
    )


def pack_kernel(quarter, features, *refs):
    steps = len(plan0[0])
    count = (len(refs) - steps - 6) // 2
    held_hbm, rows_hbm, *others_hbm = refs[: count + 2]
    *messages, held_ref, rows_ref = refs[count + 2 : count + steps + 4]
    others, (pick_ref, sems) = refs[count + steps + 4 : -2], refs[-2:]
    copies = [
        pltpu.make_async_copy(held_hbm, held_ref.at[pl.ds(0, held_hbm.shape[0])], sems.at[0]),
        pltpu.make_async_copy(rows_hbm, rows_ref, sems.at[1]),
    ]
    for index, (source, target) in enumerate(zip(others_hbm, others)):
        copies.append(pltpu.make_async_copy(source, target, sems.at[index + 2]))
    for copy in copies:
        copy.start()
    slot, odd = position(quarter)
    cells = pick_ref.shape[0]
    rows, halo, length = held_ref.shape[0] * 128 // cells, rows_ref.shape[1], messages[0].shape[0]
    held_ref[held_hbm.shape[0] :, :] = jnp.zeros(
        (held_ref.shape[0] - held_hbm.shape[0], 128), f32
    )
    copies[1].wait()
    cell = lax.broadcasted_iota(jnp.int32, (cells, halo), 0)
    for side in range(2):
        pick_ref[:, side * halo : (side + 1) * halo] = (
            cell == rows_ref[side : side + 1, :]
        ).astype(bf16)
    copies[0].wait()
    levels = features // 3

    @pl.when(slot == 0)
    def _():
        stride = -(-levels // 16) * 16
        for group, kinds in enumerate(plan0):
            heat = load_rows(held_ref, group * levels, levels, cells)
            power = power_of(heat)
            messages[kinds.index("H")][...] = to_message(
                padded(jnp.round(heat * jnp.exp2(-power[:1, :1])), stride), power, length
            )

    @pl.when(slot != 0)
    def _():
        state = load_rows(held_ref, 0, rows, cells)
        power = power_of(state)
        high, low = split(state)
        sent = dot(high, pick_ref[...]) + dot(low, pick_ref[...])
        both = halo_messages(odd, jnp.round(sent * jnp.exp2(-power[:1, :1])), power, length)
        send(plan0, slot, messages, {**both, "H": both["A"]})

    for copy in copies[2:]:
        copy.wait()


def silu(v):
    half = 0.5 * v
    return half + half * jnp.tanh(half)


def network(state, w_in_ref, b_in_ref, w_mid_ref, b_mid_ref, w_out_ref, b_out_ref):
    def bias(ref):
        return jnp.concatenate([ref[...]] * (state.shape[1] // ref.shape[1]), axis=1)

    first = silu(dot(w_in_ref[...], state) + bias(b_in_ref)).astype(bf16)
    second = silu(dot(w_mid_ref[...], first) + bias(b_mid_ref)).astype(bf16)
    return dot(w_out_ref[...], second) + bias(b_out_ref)


def first_kernel(
    w_in_t_hbm, w_mid_hbm, w_out_hbm,
    held_ref, near_ref, diff_ref, tran_ref, b_in_ref, b_mid_ref, b_out_ref,
    matrix_ref, matrix_low_ref, keep_ref, part_ref, w_in_ref, c_in_ref, c_mid_ref, c_out_ref,
    w_mid_ref, w_out_ref, w_in_t_ref, sems,
):
    sources = (w_in_t_hbm, w_mid_hbm, w_out_hbm)
    copies = [
        pltpu.make_async_copy(source, target, sems.at[index])
        for index, (source, target) in enumerate(zip(sources, (w_in_t_ref, w_mid_ref, w_out_ref)))
    ]
    for copy in copies:
        copy.start()
    rows, cells = part_ref.shape
    half_tran = 0.5 * tran_ref[...]
    weight = diff_ref[...] - half_tran
    keep = 1.0 - jnp.sum(diff_ref[...] + half_tran, axis=0, keepdims=True)
    keep_ref[...] = keep
    piece = 128
    for start in range(0, matrix_ref.shape[0], piece):
        cell = lax.broadcasted_iota(jnp.int32, (piece, cells), 0) + start
        total = jnp.zeros((piece, cells), f32)
        for edge in range(near_ref.shape[0]):
            total = total + jnp.where(
                cell == near_ref[edge : edge + 1, :], weight[edge : edge + 1, :], 0.0
            )
        matrix_ref[start : start + piece, :], matrix_low_ref[start : start + piece, :] = split(total)
    state = load_rows(held_ref, 0, rows, cells)
    high, low = split(state)
    part_ref[...] = (
        dot(high, matrix_ref[:cells, :])
        + dot(high, matrix_low_ref[:cells, :])
        + dot(low, matrix_ref[:cells, :])
        + state * keep
    )
    for copy in copies:
        copy.wait()
    features = w_in_t_ref.shape[0]
    w_in_ref[...] = jnp.zeros_like(w_in_ref)
    w_in_ref[:, :features] = w_in_t_ref[...].T
    for row_ref, column_ref in ((b_in_ref, c_in_ref), (b_mid_ref, c_mid_ref), (b_out_ref, c_out_ref)):
        column_ref[...] = jnp.broadcast_to(row_ref[...], (128, row_ref.shape[1])).T


def middle_kernel(
    quarter, received, pick_ref, part_ref, matrix_ref, matrix_low_ref,
    w_in_ref, b_in_ref, w_mid_ref, b_mid_ref, w_out_ref, b_out_ref,
    messages, state_ref,
):
    slot, odd = position(quarter)
    rows, cells = state_ref.shape
    levels, length = w_out_ref.shape[0], messages[0].shape[0]
    stride = -(-levels // 16) * 16
    heat = from_message(receive(plan0, slot, received, "H"), stride, cells // 128)[:levels]
    high, low = split(receive_halos(plan0, slot, odd, received, rows))
    state_ref[...] = (
        part_ref[...]
        + dot(high, matrix_ref[cells:, :])
        + dot(high, matrix_low_ref[cells:, :])
        + dot(low, matrix_ref[cells:, :])
    )
    state_ref[:levels, :] = state_ref[:levels, :] + heat_gain * heat
    state = state_ref[...].astype(bf16)
    sent = dot(state, pick_ref[...])
    power = power_of(sent)
    out = halo_messages(odd, jnp.round(sent * jnp.exp2(-power[:1, :1])), power, length)
    heat = network(state, w_in_ref, b_in_ref, w_mid_ref, b_mid_ref, w_out_ref, b_out_ref)
    power = power_of(heat)
    out["H"] = to_message(padded(jnp.round(heat * jnp.exp2(-power[:1, :1])), stride), power, length)
    send(plan1, slot, messages, out)


def own_kernel(
    held_ref, state_ref, matrix_ref, keep_ref,
    w_in_ref, b_in_ref, w_mid_ref, b_mid_ref, w_out_ref, b_out_ref, part_ref,
):
    rows, cells = state_ref.shape
    levels = w_out_ref.shape[0]
    start = load_rows(held_ref, 0, rows, cells).astype(bf16)
    heat = network(start, w_in_ref, b_in_ref, w_mid_ref, b_mid_ref, w_out_ref, b_out_ref)
    state = state_ref[...]
    part_ref[...] = dot(state.astype(bf16), matrix_ref[:cells, :]) + state * keep_ref[...]
    part_ref[:levels, :] = part_ref[:levels, :] + heat_gain * heat


def last_kernel(quarter, received, part_ref, matrix_ref, out_ref):
    slot, odd = position(quarter)
    rows, cells = part_ref.shape
    tiles = cells // 128
    features = out_ref.shape[0] // tiles
    levels = features // 3
    stride = -(-levels // 16) * 16

    def store_rows(first, values):
        for tile in range(tiles):
            out_ref[pl.ds(first * tiles + tile, values.shape[0], stride=tiles), :] = values[
                :, tile * 128 : (tile + 1) * 128
            ]

    @pl.when(slot == 0)
    def _():
        for group, kinds in enumerate(plan1):
            heat = from_message(received[kinds.index("H")][...], stride, tiles)
            store_rows(group * levels, heat[:levels])

    @pl.when(slot != 0)
    def _():
        halos = receive_halos(plan1, slot, odd, received, rows).astype(bf16)
        store_rows(0, (part_ref[...] + dot(halos, matrix_ref[cells:, :]))[:features])


VMEM = pl.BlockSpec(memory_space=pltpu.VMEM)
HBM = pl.BlockSpec(memory_space=pltpu.HBM)


def call(kernel, name, out_shape, *args, hbm=0, scratch=(), flops=0, limit=16 << 20):
    size = sum(a.size * a.dtype.itemsize for a in args)
    args = [
        pltpu.with_memory_space_constraint(a, pltpu.HBM) if index < hbm else a
        for index, a in enumerate(args)
    ]
    return pl.pallas_call(
        kernel,
        out_shape=out_shape,
        in_specs=[HBM] * hbm + [VMEM] * (len(args) - hbm),
        out_specs=jax.tree.map(lambda _: VMEM, out_shape),
        scratch_shapes=scratch,
        compiler_params=pltpu.CompilerParams(vmem_limit_bytes=limit),
        cost_estimate=pl.CostEstimate(flops=flops, bytes_accessed=size, transcendentals=0),
        name=name,
    )(*args)


def exchange(plan, messages, quarter, blocks):
    def partner(group, block, step):
        slot, place = group // quarter, group % quarter
        kinds = [kinds[step] for kinds in plan]
        if slot == 0 and "H" in kinds:
            return (kinds.index("H") + 1) * quarter + place, block
        kind = kinds[slot - 1] if slot else "a"
        if kind == "H":
            return place, block
        up = (block % 2 == 0) == (kind != "B")
        return group, (block + (1 if up else -1)) % blocks

    received = []
    for step, message in enumerate(messages):
        pairs = []
        for group in range(4 * quarter):
            for block in range(blocks):
                to_group, to_block = partner(group, block, step)
                pairs.append((group * blocks + block, to_group * blocks + to_block))
        received.append(lax.ppermute(message, ("grp", "blk"), pairs))
    return received


def body(held, neighbours, send_rows, diffusion, transport, w_in, b_in, w_mid, b_mid, w_out, b_out):
    quarter, blocks = lax.axis_size("grp") // 4, lax.axis_size("blk")
    _, fields, levels, cells = held.shape
    halo, hidden = send_rows.shape[1], w_mid.shape[0]
    features, tiles = fields * levels, cells // 128
    rows = -(-features // 16) * 16
    length = max(-(-levels // 16) * 16 * tiles, rows) + 16

    def shape(*dims, dtype=f32):
        return jax.ShapeDtypeStruct(dims, dtype)

    def like(array):
        return shape(*array.shape, dtype=array.dtype)

    message = shape(length, 128, dtype=i16)
    full = shape(rows, cells)
    matrix_shape = shape(cells + 2 * halo, cells, dtype=bf16)
    count0, count1 = len(plan0[0]), len(plan1[0])
    args = (neighbours, diffusion, transport, b_in[None], b_mid[None], b_out[None])
    *messages, flat, _, near, diff, tran, b_in, b_mid, b_out, pick = call(
        lambda *refs: pack_kernel(quarter, features, *refs), "pack",
        [message] * len(plan0[0])
        + [shape(rows * tiles, 128), like(send_rows)]
        + [like(array) for array in args]
        + [shape(cells, 2 * halo, dtype=bf16)],
        held.reshape(features * tiles, 128), send_rows, *args,
        hbm=2 + len(args), scratch=[pltpu.SemaphoreType.DMA((2 + len(args),))],
    )
    received = exchange(plan0, messages, quarter, blocks)
    matrix, matrix_low, keep, part1, w_in, c_in, c_mid, c_out, w_mid, w_out = call(
        first_kernel, "first",
        [
            matrix_shape, matrix_shape, shape(1, cells), full,
            shape(hidden, rows, dtype=bf16), shape(hidden, 128), shape(hidden, 128), shape(levels, 128),
            like(w_mid), like(w_out),
        ],
        w_in.T, w_mid, w_out, flat, near, diff, tran, b_in, b_mid, b_out,
        hbm=3, scratch=[pltpu.VMEM((features, hidden), bf16), pltpu.SemaphoreType.DMA((3,))],
        flops=2 * cells * hidden * hidden,
    )
    weights = (w_in, c_in, w_mid, c_mid, w_out, c_out)
    *messages, state1 = call(
        lambda *refs: middle_kernel(
            quarter, refs[:count0], *refs[count0 : count0 + 10], refs[count0 + 10 : -1], refs[-1]
        ),
        "middle", [message] * count1 + [full],
        *received, pick, part1, matrix, matrix_low, *weights, flops=2 * cells * hidden * hidden,
    )
    received = exchange(plan1, messages, quarter, blocks)
    part2 = call(
        own_kernel, "own", full, flat, state1, matrix, keep, *weights, flops=2 * cells * hidden * hidden
    )
    out = call(
        lambda *refs: last_kernel(quarter, refs[:count1], *refs[count1:]), "last",
        shape(features * tiles, 128), *received, part2, matrix, flops=2 * rows * cells * 2 * halo,
    )
    return out.reshape(held.shape)


def solution(mesh):
    placed = (
        P("grp", None, None, "blk"),
        P(None, "blk"),
        P(None, "blk"),
        P(None, "blk"),
        P(None, "blk"),
        P(),
        P(),
        P(),
        P(),
        P(),
        P(),
    )
    return jax.shard_map(
        body, mesh=mesh, in_specs=placed, out_specs=P("grp", None, None, "blk"), check_vma=False
    )
```

```python
import functools
import math

import jax
import jax.numpy as jnp
from jax import lax
from jax.experimental import pallas as pl
from jax.experimental.pallas import tpu as pltpu
from jax.sharding import PartitionSpec as P

heat_gain = 0.5
bf16, f32, i16 = jnp.bfloat16, jnp.float32, jnp.int16

plan0 = ("UDH", "UHD", "HUD")
plan1 = ("UDH", "UHD", "HUD")


def dot(a, b):
    return jnp.dot(a, b, preferred_element_type=f32)


def split(values):
    high = values.astype(bf16)
    return high, (values - high.astype(f32)).astype(bf16)


def slot_of(quarter):
    return lax.axis_index("grp") // quarter


def load_rows(ref, first, rows, cells):
    tiles = cells // 128
    return jnp.concatenate(
        [ref[pl.ds(first * tiles + tile, rows, stride=tiles), :] for tile in range(tiles)], axis=1
    )


def power_of(values):
    largest = jnp.max(jnp.abs(values), axis=0, keepdims=True)
    largest = functools.reduce(
        jnp.maximum, [largest[:, at : at + 128] for at in range(0, values.shape[1], 128)]
    )
    power = jnp.ceil(jnp.log(jnp.maximum(largest, 1e-30) * (1 / 32000)) * (1 / math.log(2)))
    return jnp.broadcast_to(power, (8, 128))


def coded(values, power):
    factor = jnp.exp2(-power[:1])
    return jnp.round(values * jnp.concatenate([factor] * (values.shape[1] // 128), axis=1))


def to_message(codes, power, length):
    tiles = [codes[:, at : at + 128] for at in range(0, codes.shape[1], 128)]
    spare = length - power.shape[0] - len(tiles) * codes.shape[0]
    if spare:
        tiles.append(jnp.zeros((spare, 128), f32))
    return jnp.concatenate([*tiles, power], axis=0).astype(jnp.int32).astype(i16)


def from_message(message, rows, tiles):
    values = message.astype(f32)
    values = values[: rows * tiles] * jnp.exp2(values[-1:])
    return jnp.concatenate([values[at * rows : (at + 1) * rows] for at in range(tiles)], axis=1)


def halo_messages(codes, power, length):
    halo = codes.shape[1] // 2
    return {
        "D": to_message(codes[:, :halo], power, length),
        "U": to_message(codes[:, halo:], power, length),
    }


def send(plan, slot, message_refs, messages):
    for step, ref in enumerate(message_refs):
        value = messages[plan[0][step]]
        for group in range(1, len(plan)):
            value = jnp.where(slot == group + 1, messages[plan[group][step]], value)
        ref[...] = value


def receive(plan, slot, message_refs, kind):
    value = message_refs[plan[0].index(kind)][...]
    for group in range(1, len(plan)):
        value = jnp.where(slot == group + 1, message_refs[plan[group].index(kind)][...], value)
    return value


def receive_halos(plan, slot, message_refs, rows):
    return jnp.concatenate(
        [from_message(receive(plan, slot, message_refs, kind), rows, 1) for kind in "UD"], axis=1
    )


def pack_kernel(quarter, features, *refs):
    steps = len(plan0[0])
    count = (len(refs) - steps - 6) // 2
    held_hbm, rows_hbm, *others_hbm = refs[: count + 2]
    *messages, held_ref, rows_ref = refs[count + 2 : count + steps + 4]
    others, (pick_ref, sems) = refs[count + steps + 4 : -2], refs[-2:]
    copies = [
        pltpu.make_async_copy(held_hbm, held_ref.at[pl.ds(0, held_hbm.shape[0])], sems.at[0]),
        pltpu.make_async_copy(rows_hbm, rows_ref, sems.at[1]),
    ]
    for index, (source, target) in enumerate(zip(others_hbm, others)):
        copies.append(pltpu.make_async_copy(source, target, sems.at[index + 2]))
    for copy in copies:
        copy.start()
    slot = slot_of(quarter)
    cells = pick_ref.shape[0]
    rows, halo, length = held_ref.shape[0] * 128 // cells, rows_ref.shape[1], messages[0].shape[0]
    held_ref[held_hbm.shape[0] :, :] = jnp.zeros(
        (held_ref.shape[0] - held_hbm.shape[0], 128), f32
    )
    copies[1].wait()
    cell = lax.broadcasted_iota(jnp.int32, (cells, halo), 0)
    for side in range(2):
        pick_ref[:, side * halo : (side + 1) * halo] = (
            cell == rows_ref[side : side + 1, :]
        ).astype(bf16)
    copies[0].wait()
    levels = features // 3

    @pl.when(slot == 0)
    def _():
        for group, kinds in enumerate(plan0):
            heat = load_rows(held_ref, group * levels, levels, cells)
            power = power_of(heat)
            messages[kinds.index("H")][...] = to_message(
                coded(heat, power), power, length
            )

    @pl.when(slot != 0)
    def _():
        state = load_rows(held_ref, 0, rows, cells)
        high, low = split(state)
        sent = dot(high, pick_ref[...]) + dot(low, pick_ref[...])
        power = power_of(sent)
        both = halo_messages(coded(sent, power), power, length)
        send(plan0, slot, messages, {**both, "H": both["U"]})

    for copy in copies[2:]:
        copy.wait()


def silu(v):
    half = 0.5 * v
    return half + half * jnp.tanh(half)


def network(state, w_in_ref, b_in_ref, w_mid_ref, b_mid_ref, w_out_ref, b_out_ref):
    def bias(ref):
        return jnp.concatenate([ref[...]] * (state.shape[1] // ref.shape[1]), axis=1)

    first = silu(dot(w_in_ref[...], state) + bias(b_in_ref)).astype(bf16)
    second = silu(dot(w_mid_ref[...], first) + bias(b_mid_ref)).astype(bf16)
    return dot(w_out_ref[...], second) + bias(b_out_ref)


def first_kernel(
    quarter, w_in_t_hbm, w_mid_hbm, w_out_hbm,
    held_ref, near_ref, diff_ref, tran_ref, b_in_ref, b_mid_ref, b_out_ref,
    matrix_ref, matrix_low_ref, keep_ref, part_ref, w_in_ref, c_in_ref, c_mid_ref, c_out_ref,
    w_mid_ref, w_out_ref, w_in_t_ref, sems,
):
    slot = slot_of(quarter)

    @pl.when(slot != 0)
    def _():
        sources = (w_in_t_hbm, w_mid_hbm, w_out_hbm)
        copies = [
            pltpu.make_async_copy(source, target, sems.at[index])
            for index, (source, target) in enumerate(zip(sources, (w_in_t_ref, w_mid_ref, w_out_ref)))
        ]
        for copy in copies:
            copy.start()
        rows, cells = part_ref.shape
        half_tran = 0.5 * tran_ref[...]
        weight = diff_ref[...] - half_tran
        keep = 1.0 - jnp.sum(diff_ref[...] + half_tran, axis=0, keepdims=True)
        keep_ref[...] = keep
        piece = 128
        for start in range(0, matrix_ref.shape[0], piece):
            cell = lax.broadcasted_iota(jnp.int32, (piece, cells), 0) + start
            total = jnp.zeros((piece, cells), f32)
            for edge in range(near_ref.shape[0]):
                total = total + jnp.where(
                    cell == near_ref[edge : edge + 1, :], weight[edge : edge + 1, :], 0.0
                )
            matrix_ref[start : start + piece, :], matrix_low_ref[start : start + piece, :] = split(total)
        state = load_rows(held_ref, 0, rows, cells)
        high, low = split(state)
        part_ref[...] = (
            dot(high, matrix_ref[:cells, :])
            + dot(high, matrix_low_ref[:cells, :])
            + dot(low, matrix_ref[:cells, :])
            + state * keep
        )
        for copy in copies:
            copy.wait()
        features = w_in_t_ref.shape[0]
        w_in_ref[...] = jnp.zeros_like(w_in_ref)
        w_in_ref[:, :features] = w_in_t_ref[...].T
        for row_ref, column_ref in ((b_in_ref, c_in_ref), (b_mid_ref, c_mid_ref), (b_out_ref, c_out_ref)):
            column_ref[...] = jnp.broadcast_to(row_ref[...], (128, row_ref.shape[1])).T


def middle_kernel(
    quarter, received, pick_ref, part_ref, matrix_ref, matrix_low_ref,
    w_in_ref, b_in_ref, w_mid_ref, b_mid_ref, w_out_ref, b_out_ref,
    messages, state_ref,
):
    slot = slot_of(quarter)
    @pl.when(slot != 0)
    def _():
        rows, cells = state_ref.shape
        levels, length = w_out_ref.shape[0], messages[0].shape[0]
        heat = from_message(receive(plan0, slot, received, "H"), levels, cells // 128)
        high, low = split(receive_halos(plan0, slot, received, rows))
        state_ref[...] = (
            part_ref[...]
            + dot(high, matrix_ref[cells:, :])
            + dot(high, matrix_low_ref[cells:, :])
            + dot(low, matrix_ref[cells:, :])
        )
        state_ref[:levels, :] = state_ref[:levels, :] + heat_gain * heat
        state = state_ref[...].astype(bf16)
        sent = dot(state, pick_ref[...])
        power = power_of(sent)
        out = halo_messages(coded(sent, power), power, length)
        heat = network(state, w_in_ref, b_in_ref, w_mid_ref, b_mid_ref, w_out_ref, b_out_ref)
        power = power_of(heat)
        out["H"] = to_message(coded(heat, power), power, length)
        send(plan1, slot, messages, out)


def own_kernel(
    quarter, held_ref, state_ref, matrix_ref, keep_ref,
    w_in_ref, b_in_ref, w_mid_ref, b_mid_ref, w_out_ref, b_out_ref, part_ref,
):
    slot = slot_of(quarter)

    @pl.when(slot != 0)
    def _():
        rows, cells = state_ref.shape
        levels = w_out_ref.shape[0]
        start = load_rows(held_ref, 0, rows, cells).astype(bf16)
        heat = network(start, w_in_ref, b_in_ref, w_mid_ref, b_mid_ref, w_out_ref, b_out_ref)
        state = state_ref[...]
        part_ref[...] = dot(state.astype(bf16), matrix_ref[:cells, :]) + state * keep_ref[...]
        part_ref[:levels, :] = part_ref[:levels, :] + heat_gain * heat


def last_kernel(quarter, received, part_ref, matrix_ref, out_ref):
    slot = slot_of(quarter)
    rows, cells = part_ref.shape
    tiles = cells // 128
    features = out_ref.shape[0] // tiles
    levels = features // 3

    def store_rows(first, values):
        for tile in range(tiles):
            out_ref[pl.ds(first * tiles + tile, values.shape[0], stride=tiles), :] = values[
                :, tile * 128 : (tile + 1) * 128
            ]

    @pl.when(slot == 0)
    def _():
        for group, kinds in enumerate(plan1):
            heat = from_message(received[kinds.index("H")][...], levels, tiles)
            store_rows(group * levels, heat)

    @pl.when(slot != 0)
    def _():
        halos = receive_halos(plan1, slot, received, rows).astype(bf16)
        store_rows(0, (part_ref[...] + dot(halos, matrix_ref[cells:, :]))[:features])


VMEM = pl.BlockSpec(memory_space=pltpu.VMEM)
HBM = pl.BlockSpec(memory_space=pltpu.HBM)


def call(kernel, name, out_shape, *args, hbm=0, scratch=(), flops=0, limit=16 << 20):
    size = sum(a.size * a.dtype.itemsize for a in args)
    args = [
        pltpu.with_memory_space_constraint(a, pltpu.HBM) if index < hbm else a
        for index, a in enumerate(args)
    ]
    return pl.pallas_call(
        kernel,
        out_shape=out_shape,
        in_specs=[HBM] * hbm + [VMEM] * (len(args) - hbm),
        out_specs=jax.tree.map(lambda _: VMEM, out_shape),
        scratch_shapes=scratch,
        compiler_params=pltpu.CompilerParams(vmem_limit_bytes=limit),
        cost_estimate=pl.CostEstimate(flops=flops, bytes_accessed=size, transcendentals=0),
        name=name,
    )(*args)


def exchange(plan, messages, quarter, blocks):
    def partner(group, block, step):
        slot, place = group // quarter, group % quarter
        kinds = [kinds[step] for kinds in plan]
        if slot == 0:
            return (kinds.index("H") + 1) * quarter + place, block
        kind = kinds[slot - 1]
        if kind == "H":
            return place, block
        return group, (block + (1 if kind == "U" else -1)) % blocks

    received = []
    for step, message in enumerate(messages):
        pairs = []
        for group in range(4 * quarter):
            for block in range(blocks):
                to_group, to_block = partner(group, block, step)
                pairs.append((group * blocks + block, to_group * blocks + to_block))
        received.append(lax.ppermute(message, ("grp", "blk"), pairs))
    return received


def body(held, neighbours, send_rows, diffusion, transport, w_in, b_in, w_mid, b_mid, w_out, b_out):
    quarter, blocks = lax.axis_size("grp") // 4, lax.axis_size("blk")
    _, fields, levels, cells = held.shape
    halo, hidden = send_rows.shape[1], w_mid.shape[0]
    features, tiles = fields * levels, cells // 128
    rows = -(-features // 16) * 16
    length = -(-(max(levels * tiles, rows) + 8) // 16) * 16

    def shape(*dims, dtype=f32):
        return jax.ShapeDtypeStruct(dims, dtype)

    def like(array):
        return shape(*array.shape, dtype=array.dtype)

    message = shape(length, 128, dtype=i16)
    full = shape(rows, cells)
    matrix_shape = shape(cells + 2 * halo, cells, dtype=bf16)
    count0, count1 = len(plan0[0]), len(plan1[0])
    args = (neighbours, diffusion, transport, b_in[None], b_mid[None], b_out[None])
    *messages, flat, _, near, diff, tran, b_in, b_mid, b_out, pick = call(
        lambda *refs: pack_kernel(quarter, features, *refs), "pack",
        [message] * len(plan0[0])
        + [shape(rows * tiles, 128), like(send_rows)]
        + [like(array) for array in args]
        + [shape(cells, 2 * halo, dtype=bf16)],
        held.reshape(features * tiles, 128), send_rows, *args,
        hbm=2 + len(args), scratch=[pltpu.SemaphoreType.DMA((2 + len(args),))],
    )
    received = exchange(plan0, messages, quarter, blocks)
    matrix, matrix_low, keep, part1, w_in, c_in, c_mid, c_out, w_mid, w_out = call(
        lambda *refs: first_kernel(quarter, *refs), "first",
        [
            matrix_shape, matrix_shape, shape(1, cells), full,
            shape(hidden, rows, dtype=bf16), shape(hidden, 128), shape(hidden, 128), shape(levels, 128),
            like(w_mid), like(w_out),
        ],
        w_in.T, w_mid, w_out, flat, near, diff, tran, b_in, b_mid, b_out,
        hbm=3, scratch=[pltpu.VMEM((features, hidden), bf16), pltpu.SemaphoreType.DMA((3,))],
        flops=2 * cells * hidden * hidden,
    )
    weights = (w_in, c_in, w_mid, c_mid, w_out, c_out)
    *messages, state1 = call(
        lambda *refs: middle_kernel(
            quarter, refs[:count0], *refs[count0 : count0 + 10], refs[count0 + 10 : -1], refs[-1]
        ),
        "middle", [message] * count1 + [full],
        *received, pick, part1, matrix, matrix_low, *weights, flops=2 * cells * hidden * hidden,
    )
    received = exchange(plan1, messages, quarter, blocks)
    part2 = call(
        lambda *refs: own_kernel(quarter, *refs), "own", full, flat, state1, matrix, keep, *weights, flops=2 * cells * hidden * hidden
    )
    out = call(
        lambda *refs: last_kernel(quarter, refs[:count1], *refs[count1:]), "last",
        shape(features * tiles, 128), *received, part2, matrix, flops=2 * rows * cells * 2 * halo,
    )
    return out.reshape(held.shape)


def solution(mesh):
    placed = (
        P("grp", None, None, "blk"),
        P(None, "blk"),
        P(None, "blk"),
        P(None, "blk"),
        P(None, "blk"),
        P(),
        P(),
        P(),
        P(),
        P(),
        P(),
    )
    return jax.shard_map(
        body, mesh=mesh, in_specs=placed, out_specs=P("grp", None, None, "blk"), check_vma=False
    )
```

```python
import functools
import math

import jax
import jax.numpy as jnp
from jax import lax
from jax.experimental import pallas as pl
from jax.experimental.pallas import tpu as pltpu
from jax.sharding import PartitionSpec as P

heat_gain = 0.5
bf16, f32, i16 = jnp.bfloat16, jnp.float32, jnp.int16

plan0 = ("UDH", "UHD", "HUD")
plan1 = ("UDH", "UHD", "HUD")


def dot(a, b):
    return jnp.dot(a, b, preferred_element_type=f32)


def split(values):
    high = values.astype(bf16)
    return high, (values - high.astype(f32)).astype(bf16)


def slot_of(quarter):
    return lax.axis_index("grp") // quarter


def load_rows(ref, first, rows, cells):
    tiles = cells // 128
    return jnp.concatenate(
        [ref[pl.ds(first * tiles + tile, rows, stride=tiles), :] for tile in range(tiles)], axis=1
    )


def power_of(values):
    largest = jnp.max(jnp.abs(values), axis=0, keepdims=True)
    largest = functools.reduce(
        jnp.maximum, [largest[:, at : at + 128] for at in range(0, values.shape[1], 128)]
    )
    power = jnp.ceil(jnp.log(jnp.maximum(largest, 1e-30) * (1 / 32000)) * (1 / math.log(2)))
    return jnp.broadcast_to(power, (8, 128))


def coded(values, power):
    factor = jnp.exp2(-power[:1])
    return jnp.round(values * jnp.concatenate([factor] * (values.shape[1] // 128), axis=1))


def to_message(codes, power, length):
    tiles = [codes[:, at : at + 128] for at in range(0, codes.shape[1], 128)]
    spare = length - power.shape[0] - len(tiles) * codes.shape[0]
    if spare:
        tiles.append(jnp.zeros((spare, 128), f32))
    return jnp.concatenate([*tiles, power], axis=0).astype(jnp.int32).astype(i16)


def from_message(message, rows, tiles):
    values = message.astype(f32)
    values = values[: rows * tiles] * jnp.exp2(values[-1:])
    return jnp.concatenate([values[at * rows : (at + 1) * rows] for at in range(tiles)], axis=1)


def halo_messages(codes, power, length):
    halo = codes.shape[1] // 2
    return {
        "D": to_message(codes[:, :halo], power, length),
        "U": to_message(codes[:, halo:], power, length),
    }


def send(plan, slot, message_refs, messages):
    for step, ref in enumerate(message_refs):
        value = messages[plan[0][step]]
        for group in range(1, len(plan)):
            value = jnp.where(slot == group + 1, messages[plan[group][step]], value)
        ref[...] = value


def receive(plan, slot, message_refs, kind):
    value = message_refs[plan[0].index(kind)][...]
    for group in range(1, len(plan)):
        value = jnp.where(slot == group + 1, message_refs[plan[group].index(kind)][...], value)
    return value


def receive_halos(plan, slot, message_refs, rows):
    return jnp.concatenate(
        [from_message(receive(plan, slot, message_refs, kind), rows, 1) for kind in "UD"], axis=1
    )


def pack_kernel(quarter, features, *refs):
    steps = len(plan0[0])
    count = (len(refs) - steps - 6) // 2
    held_hbm, rows_hbm, *others_hbm = refs[: count + 2]
    *messages, held_ref, rows_ref = refs[count + 2 : count + steps + 4]
    others, (pick_ref, sems) = refs[count + steps + 4 : -2], refs[-2:]
    copies = [
        pltpu.make_async_copy(held_hbm, held_ref.at[pl.ds(0, held_hbm.shape[0])], sems.at[0]),
        pltpu.make_async_copy(rows_hbm, rows_ref, sems.at[1]),
    ]
    for index, (source, target) in enumerate(zip(others_hbm, others)):
        copies.append(pltpu.make_async_copy(source, target, sems.at[index + 2]))
    for copy in copies:
        copy.start()
    slot = slot_of(quarter)
    cells = pick_ref.shape[0]
    rows, halo, length = held_ref.shape[0] * 128 // cells, rows_ref.shape[1], messages[0].shape[0]
    held_ref[held_hbm.shape[0] :, :] = jnp.zeros(
        (held_ref.shape[0] - held_hbm.shape[0], 128), f32
    )
    copies[1].wait()
    cell = lax.broadcasted_iota(jnp.int32, (cells, halo), 0)
    for side in range(2):
        pick_ref[:, side * halo : (side + 1) * halo] = (
            cell == rows_ref[side : side + 1, :]
        ).astype(bf16)
    copies[0].wait()
    levels = features // 3

    @pl.when(slot == 0)
    def _():
        for group, kinds in enumerate(plan0):
            heat = load_rows(held_ref, group * levels, levels, cells)
            power = power_of(heat)
            messages[kinds.index("H")][...] = to_message(
                coded(heat, power), power, length
            )

    @pl.when(slot != 0)
    def _():
        state = load_rows(held_ref, 0, rows, cells)
        sent = dot(state.astype(bf16), pick_ref[...])
        power = power_of(sent)
        both = halo_messages(coded(sent, power), power, length)
        send(plan0, slot, messages, {**both, "H": both["U"]})

    for copy in copies[2:]:
        copy.wait()


def silu(v):
    half = 0.5 * v
    return half + half * jnp.tanh(half)


def network(state, w_in_ref, b_in_ref, w_mid_ref, b_mid_ref, w_out_ref, b_out_ref):
    def bias(ref):
        return jnp.concatenate([ref[...]] * (state.shape[1] // ref.shape[1]), axis=1)

    first = silu(dot(w_in_ref[...], state) + bias(b_in_ref)).astype(bf16)
    second = silu(dot(w_mid_ref[...], first) + bias(b_mid_ref)).astype(bf16)
    return dot(w_out_ref[...], second) + bias(b_out_ref)


def first_kernel(
    quarter, w_in_t_hbm, w_mid_hbm, w_out_hbm,
    held_ref, near_ref, diff_ref, tran_ref, b_in_ref, b_mid_ref, b_out_ref,
    matrix_ref, matrix_low_ref, keep_ref, part_ref, w_in_ref, c_in_ref, c_mid_ref, c_out_ref,
    w_mid_ref, w_out_ref, w_in_t_ref, sems,
):
    slot = slot_of(quarter)

    @pl.when(slot != 0)
    def _():
        sources = (w_in_t_hbm, w_mid_hbm, w_out_hbm)
        copies = [
            pltpu.make_async_copy(source, target, sems.at[index])
            for index, (source, target) in enumerate(zip(sources, (w_in_t_ref, w_mid_ref, w_out_ref)))
        ]
        for copy in copies:
            copy.start()
        rows, cells = part_ref.shape
        half_tran = 0.5 * tran_ref[...]
        weight = diff_ref[...] - half_tran
        keep = 1.0 - jnp.sum(diff_ref[...] + half_tran, axis=0, keepdims=True)
        keep_ref[...] = keep
        piece = 128
        for start in range(0, matrix_ref.shape[0], piece):
            cell = lax.broadcasted_iota(jnp.int32, (piece, cells), 0) + start
            total = jnp.zeros((piece, cells), f32)
            for edge in range(near_ref.shape[0]):
                total = total + jnp.where(
                    cell == near_ref[edge : edge + 1, :], weight[edge : edge + 1, :], 0.0
                )
            high, low = split(total)
            matrix_ref[start : start + piece, :] = high
            if start < cells:
                matrix_low_ref[start : start + piece, :] = low
        state = load_rows(held_ref, 0, rows, cells)
        high, low = split(state)
        part_ref[...] = (
            dot(high, matrix_ref[:cells, :])
            + dot(high, matrix_low_ref[...])
            + dot(low, matrix_ref[:cells, :])
            + state * keep
        )
        for copy in copies:
            copy.wait()
        features = w_in_t_ref.shape[0]
        w_in_ref[...] = jnp.zeros_like(w_in_ref)
        w_in_ref[:, :features] = w_in_t_ref[...].T
        for row_ref, column_ref in ((b_in_ref, c_in_ref), (b_mid_ref, c_mid_ref), (b_out_ref, c_out_ref)):
            column_ref[...] = jnp.broadcast_to(row_ref[...], (128, row_ref.shape[1])).T


def middle_kernel(
    quarter, received, pick_ref, part_ref, matrix_ref,
    w_in_ref, b_in_ref, w_mid_ref, b_mid_ref, w_out_ref, b_out_ref,
    messages, state_ref,
):
    slot = slot_of(quarter)
    @pl.when(slot != 0)
    def _():
        rows, cells = state_ref.shape
        levels, length = w_out_ref.shape[0], messages[0].shape[0]
        heat = from_message(receive(plan0, slot, received, "H"), levels, cells // 128)
        halos = receive_halos(plan0, slot, received, rows).astype(bf16)
        state_ref[...] = part_ref[...] + dot(halos, matrix_ref[cells:, :])
        state_ref[:levels, :] = state_ref[:levels, :] + heat_gain * heat
        state = state_ref[...].astype(bf16)
        sent = dot(state, pick_ref[...])
        power = power_of(sent)
        out = halo_messages(coded(sent, power), power, length)
        heat = network(state, w_in_ref, b_in_ref, w_mid_ref, b_mid_ref, w_out_ref, b_out_ref)
        power = power_of(heat)
        out["H"] = to_message(coded(heat, power), power, length)
        send(plan1, slot, messages, out)


def own_kernel(
    quarter, held_ref, state_ref, matrix_ref, matrix_low_ref, keep_ref,
    w_in_ref, b_in_ref, w_mid_ref, b_mid_ref, w_out_ref, b_out_ref, part_ref,
):
    slot = slot_of(quarter)

    @pl.when(slot != 0)
    def _():
        rows, cells = state_ref.shape
        levels = w_out_ref.shape[0]
        start = load_rows(held_ref, 0, rows, cells).astype(bf16)
        heat = network(start, w_in_ref, b_in_ref, w_mid_ref, b_mid_ref, w_out_ref, b_out_ref)
        state = state_ref[...]
        high = state.astype(bf16)
        part_ref[...] = (
            dot(high, matrix_ref[:cells, :]) + dot(high, matrix_low_ref[...]) + state * keep_ref[...]
        )
        part_ref[:levels, :] = part_ref[:levels, :] + heat_gain * heat


def last_kernel(quarter, received, part_ref, matrix_ref, out_ref):
    slot = slot_of(quarter)
    rows, cells = part_ref.shape
    tiles = cells // 128
    features = out_ref.shape[0] // tiles
    levels = features // 3

    def store_rows(first, values):
        for tile in range(tiles):
            out_ref[pl.ds(first * tiles + tile, values.shape[0], stride=tiles), :] = values[
                :, tile * 128 : (tile + 1) * 128
            ]

    @pl.when(slot == 0)
    def _():
        for group, kinds in enumerate(plan1):
            heat = from_message(received[kinds.index("H")][...], levels, tiles)
            store_rows(group * levels, heat)

    @pl.when(slot != 0)
    def _():
        halos = receive_halos(plan1, slot, received, rows).astype(bf16)
        store_rows(0, (part_ref[...] + dot(halos, matrix_ref[cells:, :]))[:features])


VMEM = pl.BlockSpec(memory_space=pltpu.VMEM)
HBM = pl.BlockSpec(memory_space=pltpu.HBM)


def call(kernel, name, out_shape, *args, hbm=0, scratch=(), flops=0, limit=16 << 20):
    size = sum(a.size * a.dtype.itemsize for a in args)
    args = [
        pltpu.with_memory_space_constraint(a, pltpu.HBM) if index < hbm else a
        for index, a in enumerate(args)
    ]
    return pl.pallas_call(
        kernel,
        out_shape=out_shape,
        in_specs=[HBM] * hbm + [VMEM] * (len(args) - hbm),
        out_specs=jax.tree.map(lambda _: VMEM, out_shape),
        scratch_shapes=scratch,
        compiler_params=pltpu.CompilerParams(vmem_limit_bytes=limit),
        cost_estimate=pl.CostEstimate(flops=flops, bytes_accessed=size, transcendentals=0),
        name=name,
    )(*args)


def exchange(plan, messages, quarter, blocks):
    def partner(group, block, step):
        slot, place = group // quarter, group % quarter
        kinds = [kinds[step] for kinds in plan]
        if slot == 0:
            return (kinds.index("H") + 1) * quarter + place, block
        kind = kinds[slot - 1]
        if kind == "H":
            return place, block
        return group, (block + (1 if kind == "U" else -1)) % blocks

    received = []
    for step, message in enumerate(messages):
        pairs = []
        for group in range(4 * quarter):
            for block in range(blocks):
                to_group, to_block = partner(group, block, step)
                pairs.append((group * blocks + block, to_group * blocks + to_block))
        received.append(lax.ppermute(message, ("grp", "blk"), pairs))
    return received


def body(held, neighbours, send_rows, diffusion, transport, w_in, b_in, w_mid, b_mid, w_out, b_out):
    quarter, blocks = lax.axis_size("grp") // 4, lax.axis_size("blk")
    _, fields, levels, cells = held.shape
    halo, hidden = send_rows.shape[1], w_mid.shape[0]
    features, tiles = fields * levels, cells // 128
    rows = -(-features // 16) * 16
    length = -(-(max(levels * tiles, rows) + 8) // 16) * 16

    def shape(*dims, dtype=f32):
        return jax.ShapeDtypeStruct(dims, dtype)

    def like(array):
        return shape(*array.shape, dtype=array.dtype)

    message = shape(length, 128, dtype=i16)
    full = shape(rows, cells)
    matrix_shape = shape(cells + 2 * halo, cells, dtype=bf16)
    count0, count1 = len(plan0[0]), len(plan1[0])
    args = (neighbours, diffusion, transport, b_in[None], b_mid[None], b_out[None])
    *messages, flat, _, near, diff, tran, b_in, b_mid, b_out, pick = call(
        lambda *refs: pack_kernel(quarter, features, *refs), "pack",
        [message] * len(plan0[0])
        + [shape(rows * tiles, 128), like(send_rows)]
        + [like(array) for array in args]
        + [shape(cells, 2 * halo, dtype=bf16)],
        held.reshape(features * tiles, 128), send_rows, *args,
        hbm=2 + len(args), scratch=[pltpu.SemaphoreType.DMA((2 + len(args),))],
    )
    received = exchange(plan0, messages, quarter, blocks)
    matrix, matrix_low, keep, part1, w_in, c_in, c_mid, c_out, w_mid, w_out = call(
        lambda *refs: first_kernel(quarter, *refs), "first",
        [
            matrix_shape, shape(cells, cells, dtype=bf16), shape(1, cells), full,
            shape(hidden, rows, dtype=bf16), shape(hidden, 128), shape(hidden, 128), shape(levels, 128),
            like(w_mid), like(w_out),
        ],
        w_in.T, w_mid, w_out, flat, near, diff, tran, b_in, b_mid, b_out,
        hbm=3, scratch=[
            pltpu.VMEM((features, hidden), bf16), pltpu.SemaphoreType.DMA((3,)),
        ],
        flops=2 * cells * hidden * hidden,
    )
    weights = (w_in, c_in, w_mid, c_mid, w_out, c_out)
    *messages, state1 = call(
        lambda *refs: middle_kernel(
            quarter, refs[:count0], *refs[count0 : count0 + 9], refs[count0 + 9 : -1], refs[-1]
        ),
        "middle", [message] * count1 + [full],
        *received, pick, part1, matrix, *weights, flops=2 * cells * hidden * hidden,
    )
    received = exchange(plan1, messages, quarter, blocks)
    part2 = call(
        lambda *refs: own_kernel(quarter, *refs), "own", full, flat, state1, matrix, matrix_low, keep, *weights, flops=2 * cells * hidden * hidden
    )
    out = call(
        lambda *refs: last_kernel(quarter, refs[:count1], *refs[count1:]), "last",
        shape(features * tiles, 128), *received, part2, matrix, flops=2 * rows * cells * 2 * halo,
    )
    return out.reshape(held.shape)


def solution(mesh):
    placed = (
        P("grp", None, None, "blk"),
        P(None, "blk"),
        P(None, "blk"),
        P(None, "blk"),
        P(None, "blk"),
        P(),
        P(),
        P(),
        P(),
        P(),
        P(),
    )
    return jax.shard_map(
        body, mesh=mesh, in_specs=placed, out_specs=P("grp", None, None, "blk"), check_vma=False
    )
```

```python
import functools
import math

import jax
import jax.numpy as jnp
from jax import lax
from jax.experimental import pallas as pl
from jax.experimental.pallas import tpu as pltpu
from jax.sharding import PartitionSpec as P

heat_gain = 0.5
bf16, f32, i16 = jnp.bfloat16, jnp.float32, jnp.int16

plan0 = ("UDH", "UHD", "HUD")
plan1 = ("UDH", "UHD", "HUD")


def dot(a, b):
    return jnp.dot(a, b, preferred_element_type=f32)


def split(values):
    high = values.astype(bf16)
    return high, (values - high.astype(f32)).astype(bf16)


def slot_of(quarter):
    return lax.axis_index("grp") // quarter


def load_rows(ref, first, rows, cells):
    tiles = cells // 128
    return jnp.concatenate(
        [ref[pl.ds(first * tiles + tile, rows, stride=tiles), :] for tile in range(tiles)], axis=1
    )


def power_of(values):
    largest = jnp.max(jnp.abs(values), axis=0, keepdims=True)
    largest = functools.reduce(
        jnp.maximum, [largest[:, at : at + 128] for at in range(0, values.shape[1], 128)]
    )
    power = jnp.ceil(jnp.log(jnp.maximum(largest, 1e-30) * (1 / 32000)) * (8 / math.log(2)))
    return jnp.broadcast_to(power, (8, 128))


def coded(values, power):
    factor = jnp.exp2(power[:1] * (-1 / 8))
    return jnp.round(values * jnp.concatenate([factor] * (values.shape[1] // 128), axis=1))


def to_message(codes, power, length):
    tiles = [codes[:, at : at + 128] for at in range(0, codes.shape[1], 128)]
    spare = length - power.shape[0] - len(tiles) * codes.shape[0]
    if spare:
        tiles.append(jnp.zeros((spare, 128), f32))
    return jnp.concatenate([*tiles, power], axis=0).astype(jnp.int32).astype(i16)


def from_message(message, rows, tiles):
    values = message.astype(f32)
    values = values[: rows * tiles] * jnp.exp2(values[-1:] * (1 / 8))
    return jnp.concatenate([values[at * rows : (at + 1) * rows] for at in range(tiles)], axis=1)


def halo_messages(codes, power, length):
    halo = codes.shape[1] // 2
    return {
        "D": to_message(codes[:, :halo], power, length),
        "U": to_message(codes[:, halo:], power, length),
    }


def send(plan, slot, message_refs, messages):
    for step, ref in enumerate(message_refs):
        value = messages[plan[0][step]]
        for group in range(1, len(plan)):
            value = jnp.where(slot == group + 1, messages[plan[group][step]], value)
        ref[...] = value


def receive(plan, slot, message_refs, kind):
    value = message_refs[plan[0].index(kind)][...]
    for group in range(1, len(plan)):
        value = jnp.where(slot == group + 1, message_refs[plan[group].index(kind)][...], value)
    return value


def receive_halos(plan, slot, message_refs, rows):
    return jnp.concatenate(
        [from_message(receive(plan, slot, message_refs, kind), rows, 1) for kind in "UD"], axis=1
    )


def pack_kernel(quarter, features, *refs):
    steps = len(plan0[0])
    count = (len(refs) - steps - 6) // 2
    held_hbm, rows_hbm, *others_hbm = refs[: count + 2]
    *messages, held_ref, rows_ref = refs[count + 2 : count + steps + 4]
    others, (pick_ref, sems) = refs[count + steps + 4 : -2], refs[-2:]
    copies = [
        pltpu.make_async_copy(held_hbm, held_ref.at[pl.ds(0, held_hbm.shape[0])], sems.at[0]),
        pltpu.make_async_copy(rows_hbm, rows_ref, sems.at[1]),
    ]
    for index, (source, target) in enumerate(zip(others_hbm, others)):
        copies.append(pltpu.make_async_copy(source, target, sems.at[index + 2]))
    for copy in copies:
        copy.start()
    slot = slot_of(quarter)
    cells = pick_ref.shape[0]
    rows, halo, length = held_ref.shape[0] * 128 // cells, rows_ref.shape[1], messages[0].shape[0]
    held_ref[held_hbm.shape[0] :, :] = jnp.zeros(
        (held_ref.shape[0] - held_hbm.shape[0], 128), f32
    )
    copies[1].wait()
    cell = lax.broadcasted_iota(jnp.int32, (cells, halo), 0)
    for side in range(2):
        pick_ref[:, side * halo : (side + 1) * halo] = (
            cell == rows_ref[side : side + 1, :]
        ).astype(bf16)
    copies[0].wait()
    levels = features // 3

    @pl.when(slot == 0)
    def _():
        for group, kinds in enumerate(plan0):
            heat = load_rows(held_ref, group * levels, levels, cells)
            power = power_of(heat)
            messages[kinds.index("H")][...] = to_message(
                coded(heat, power), power, length
            )

    @pl.when(slot != 0)
    def _():
        state = load_rows(held_ref, 0, rows, cells)
        high, low = split(state)
        sent = dot(high, pick_ref[...]) + dot(low, pick_ref[...])
        power = power_of(sent)
        both = halo_messages(coded(sent, power), power, length)
        send(plan0, slot, messages, {**both, "H": both["U"]})

    for copy in copies[2:]:
        copy.wait()


def silu(v):
    half = 0.5 * v
    return half + half * jnp.tanh(half)


def network(state, w_in_ref, b_in_ref, w_mid_ref, b_mid_ref, w_out_ref, b_out_ref):
    def bias(ref):
        return jnp.concatenate([ref[...]] * (state.shape[1] // ref.shape[1]), axis=1)

    first = silu(dot(w_in_ref[...], state) + bias(b_in_ref)).astype(bf16)
    second = silu(dot(w_mid_ref[...], first) + bias(b_mid_ref)).astype(bf16)
    return dot(w_out_ref[...], second) + bias(b_out_ref)


def first_kernel(
    quarter, w_in_t_hbm, w_mid_hbm, w_out_hbm,
    held_ref, near_ref, diff_ref, tran_ref, b_in_ref, b_mid_ref, b_out_ref,
    matrix_ref, matrix_low_ref, keep_ref, part_ref, w_in_ref, c_in_ref, c_mid_ref, c_out_ref,
    w_mid_ref, w_out_ref, w_in_t_ref, sems,
):
    slot = slot_of(quarter)

    @pl.when(slot != 0)
    def _():
        sources = (w_in_t_hbm, w_mid_hbm, w_out_hbm)
        copies = [
            pltpu.make_async_copy(source, target, sems.at[index])
            for index, (source, target) in enumerate(zip(sources, (w_in_t_ref, w_mid_ref, w_out_ref)))
        ]
        for copy in copies:
            copy.start()
        rows, cells = part_ref.shape
        half_tran = 0.5 * tran_ref[...]
        weight = diff_ref[...] - half_tran
        keep = 1.0 - jnp.sum(diff_ref[...] + half_tran, axis=0, keepdims=True)
        keep_ref[...] = keep
        piece = 128
        for start in range(0, matrix_ref.shape[0], piece):
            cell = lax.broadcasted_iota(jnp.int32, (piece, cells), 0) + start
            total = jnp.zeros((piece, cells), f32)
            for edge in range(near_ref.shape[0]):
                total = total + jnp.where(
                    cell == near_ref[edge : edge + 1, :], weight[edge : edge + 1, :], 0.0
                )
            matrix_ref[start : start + piece, :], matrix_low_ref[start : start + piece, :] = split(total)
        state = load_rows(held_ref, 0, rows, cells)
        high, low = split(state)
        part_ref[...] = (
            dot(high, matrix_ref[:cells, :])
            + dot(high, matrix_low_ref[:cells, :])
            + dot(low, matrix_ref[:cells, :])
            + state * keep
        )
        for copy in copies:
            copy.wait()
        features = w_in_t_ref.shape[0]
        w_in_ref[...] = jnp.zeros_like(w_in_ref)
        w_in_ref[:, :features] = w_in_t_ref[...].T
        for row_ref, column_ref in ((b_in_ref, c_in_ref), (b_mid_ref, c_mid_ref), (b_out_ref, c_out_ref)):
            column_ref[...] = jnp.broadcast_to(row_ref[...], (128, row_ref.shape[1])).T


def middle_kernel(
    quarter, received, pick_ref, part_ref, matrix_ref, matrix_low_ref,
    w_in_ref, b_in_ref, w_mid_ref, b_mid_ref, w_out_ref, b_out_ref,
    messages, state_ref,
):
    slot = slot_of(quarter)
    @pl.when(slot != 0)
    def _():
        rows, cells = state_ref.shape
        levels, length = w_out_ref.shape[0], messages[0].shape[0]
        heat = from_message(receive(plan0, slot, received, "H"), levels, cells // 128)
        high, low = split(receive_halos(plan0, slot, received, rows))
        state_ref[...] = (
            part_ref[...]
            + dot(high, matrix_ref[cells:, :])
            + dot(high, matrix_low_ref[cells:, :])
            + dot(low, matrix_ref[cells:, :])
        )
        state_ref[:levels, :] = state_ref[:levels, :] + heat_gain * heat
        state = state_ref[...].astype(bf16)
        sent = dot(state, pick_ref[...])
        power = power_of(sent)
        out = halo_messages(coded(sent, power), power, length)
        heat = network(state, w_in_ref, b_in_ref, w_mid_ref, b_mid_ref, w_out_ref, b_out_ref)
        power = power_of(heat)
        out["H"] = to_message(coded(heat, power), power, length)
        send(plan1, slot, messages, out)


def own_kernel(
    quarter, held_ref, state_ref, matrix_ref, keep_ref,
    w_in_ref, b_in_ref, w_mid_ref, b_mid_ref, w_out_ref, b_out_ref, part_ref,
):
    slot = slot_of(quarter)

    @pl.when(slot != 0)
    def _():
        rows, cells = state_ref.shape
        levels = w_out_ref.shape[0]
        start = load_rows(held_ref, 0, rows, cells).astype(bf16)
        heat = network(start, w_in_ref, b_in_ref, w_mid_ref, b_mid_ref, w_out_ref, b_out_ref)
        state = state_ref[...]
        part_ref[...] = dot(state.astype(bf16), matrix_ref[:cells, :]) + state * keep_ref[...]
        part_ref[:levels, :] = part_ref[:levels, :] + heat_gain * heat


def last_kernel(quarter, received, part_ref, matrix_ref, out_ref):
    slot = slot_of(quarter)
    rows, cells = part_ref.shape
    tiles = cells // 128
    features = out_ref.shape[0] // tiles
    levels = features // 3

    def store_rows(first, values):
        for tile in range(tiles):
            out_ref[pl.ds(first * tiles + tile, values.shape[0], stride=tiles), :] = values[
                :, tile * 128 : (tile + 1) * 128
            ]

    @pl.when(slot == 0)
    def _():
        for group, kinds in enumerate(plan1):
            heat = from_message(received[kinds.index("H")][...], levels, tiles)
            store_rows(group * levels, heat)

    @pl.when(slot != 0)
    def _():
        halos = receive_halos(plan1, slot, received, rows).astype(bf16)
        store_rows(0, (part_ref[...] + dot(halos, matrix_ref[cells:, :]))[:features])


VMEM = pl.BlockSpec(memory_space=pltpu.VMEM)
HBM = pl.BlockSpec(memory_space=pltpu.HBM)


def call(kernel, name, out_shape, *args, hbm=0, scratch=(), flops=0, limit=16 << 20):
    size = sum(a.size * a.dtype.itemsize for a in args)
    args = [
        pltpu.with_memory_space_constraint(a, pltpu.HBM) if index < hbm else a
        for index, a in enumerate(args)
    ]
    return pl.pallas_call(
        kernel,
        out_shape=out_shape,
        in_specs=[HBM] * hbm + [VMEM] * (len(args) - hbm),
        out_specs=jax.tree.map(lambda _: VMEM, out_shape),
        scratch_shapes=scratch,
        compiler_params=pltpu.CompilerParams(vmem_limit_bytes=limit),
        cost_estimate=pl.CostEstimate(flops=flops, bytes_accessed=size, transcendentals=0),
        name=name,
    )(*args)


def exchange(plan, messages, quarter, blocks):
    def partner(group, block, step):
        slot, place = group // quarter, group % quarter
        kinds = [kinds[step] for kinds in plan]
        if slot == 0:
            return (kinds.index("H") + 1) * quarter + place, block
        kind = kinds[slot - 1]
        if kind == "H":
            return place, block
        return group, (block + (1 if kind == "U" else -1)) % blocks

    received = []
    for step, message in enumerate(messages):
        pairs = []
        for group in range(4 * quarter):
            for block in range(blocks):
                to_group, to_block = partner(group, block, step)
                pairs.append((group * blocks + block, to_group * blocks + to_block))
        received.append(lax.ppermute(message, ("grp", "blk"), pairs))
    return received


def body(held, neighbours, send_rows, diffusion, transport, w_in, b_in, w_mid, b_mid, w_out, b_out):
    quarter, blocks = lax.axis_size("grp") // 4, lax.axis_size("blk")
    _, fields, levels, cells = held.shape
    halo, hidden = send_rows.shape[1], w_mid.shape[0]
    features, tiles = fields * levels, cells // 128
    rows = -(-features // 16) * 16
    length = -(-(max(levels * tiles, rows) + 8) // 16) * 16

    def shape(*dims, dtype=f32):
        return jax.ShapeDtypeStruct(dims, dtype)

    def like(array):
        return shape(*array.shape, dtype=array.dtype)

    message = shape(length, 128, dtype=i16)
    full = shape(rows, cells)
    matrix_shape = shape(cells + 2 * halo, cells, dtype=bf16)
    count0, count1 = len(plan0[0]), len(plan1[0])
    args = (neighbours, diffusion, transport, b_in[None], b_mid[None], b_out[None])
    *messages, flat, _, near, diff, tran, b_in, b_mid, b_out, pick = call(
        lambda *refs: pack_kernel(quarter, features, *refs), "pack",
        [message] * len(plan0[0])
        + [shape(rows * tiles, 128), like(send_rows)]
        + [like(array) for array in args]
        + [shape(cells, 2 * halo, dtype=bf16)],
        held.reshape(features * tiles, 128), send_rows, *args,
        hbm=2 + len(args), scratch=[pltpu.SemaphoreType.DMA((2 + len(args),))],
    )
    received = exchange(plan0, messages, quarter, blocks)
    matrix, matrix_low, keep, part1, w_in, c_in, c_mid, c_out, w_mid, w_out = call(
        lambda *refs: first_kernel(quarter, *refs), "first",
        [
            matrix_shape, matrix_shape, shape(1, cells), full,
            shape(hidden, rows, dtype=bf16), shape(hidden, 128), shape(hidden, 128), shape(levels, 128),
            like(w_mid), like(w_out),
        ],
        w_in.T, w_mid, w_out, flat, near, diff, tran, b_in, b_mid, b_out,
        hbm=3, scratch=[pltpu.VMEM((features, hidden), bf16), pltpu.SemaphoreType.DMA((3,))],
        flops=2 * cells * hidden * hidden,
    )
    weights = (w_in, c_in, w_mid, c_mid, w_out, c_out)
    *messages, state1 = call(
        lambda *refs: middle_kernel(
            quarter, refs[:count0], *refs[count0 : count0 + 10], refs[count0 + 10 : -1], refs[-1]
        ),
        "middle", [message] * count1 + [full],
        *received, pick, part1, matrix, matrix_low, *weights, flops=2 * cells * hidden * hidden,
    )
    received = exchange(plan1, messages, quarter, blocks)
    part2 = call(
        lambda *refs: own_kernel(quarter, *refs), "own", full, flat, state1, matrix, keep, *weights, flops=2 * cells * hidden * hidden
    )
    out = call(
        lambda *refs: last_kernel(quarter, refs[:count1], *refs[count1:]), "last",
        shape(features * tiles, 128), *received, part2, matrix, flops=2 * rows * cells * 2 * halo,
    )
    return out.reshape(held.shape)


def solution(mesh):
    placed = (
        P("grp", None, None, "blk"),
        P(None, "blk"),
        P(None, "blk"),
        P(None, "blk"),
        P(None, "blk"),
        P(),
        P(),
        P(),
        P(),
        P(),
        P(),
    )
    return jax.shard_map(
        body, mesh=mesh, in_specs=placed, out_specs=P("grp", None, None, "blk"), check_vma=False
    )
```

```python
import functools
import math

import jax
import jax.numpy as jnp
from jax import lax
from jax.experimental import pallas as pl
from jax.experimental.pallas import tpu as pltpu
from jax.sharding import PartitionSpec as P

heat_gain = 0.5
bf16, f32, i16 = jnp.bfloat16, jnp.float32, jnp.int16

plan0 = ("UDH", "UHD", "HUD")
plan1 = ("UDH", "UHD", "HUD")


def dot(a, b):
    return jnp.dot(a, b, preferred_element_type=f32)


def split(values):
    high = values.astype(bf16)
    return high, (values - high.astype(f32)).astype(bf16)


def slot_of(quarter):
    return lax.axis_index("grp") // quarter


def load_rows(ref, first, rows, cells):
    tiles = cells // 128
    return jnp.concatenate(
        [ref[pl.ds(first * tiles + tile, rows, stride=tiles), :] for tile in range(tiles)], axis=1
    )


def power_of(values):
    largest = jnp.max(jnp.abs(values), axis=0, keepdims=True)
    largest = functools.reduce(
        jnp.maximum, [largest[:, at : at + 128] for at in range(0, values.shape[1], 128)]
    )
    power = jnp.ceil(jnp.log(jnp.maximum(largest, 1e-30) * (1 / 32000)) * (8 / math.log(2)))
    return jnp.broadcast_to(power, (8, 128))


def coded(values, power):
    factor = jnp.exp2(power[:1] * (-1 / 8))
    return jnp.round(values * jnp.concatenate([factor] * (values.shape[1] // 128), axis=1))


def to_message(codes, power, length):
    tiles = [codes[:, at : at + 128] for at in range(0, codes.shape[1], 128)]
    spare = length - power.shape[0] - len(tiles) * codes.shape[0]
    if spare:
        tiles.append(jnp.zeros((spare, 128), f32))
    return jnp.concatenate([*tiles, power], axis=0).astype(jnp.int32).astype(i16)


def from_message(message, rows, tiles):
    values = message.astype(f32)
    values = values[: rows * tiles] * jnp.exp2(values[-1:] * (1 / 8))
    return jnp.concatenate([values[at * rows : (at + 1) * rows] for at in range(tiles)], axis=1)


def halo_messages(codes, power, length):
    halo = codes.shape[1] // 2
    return {
        "D": to_message(codes[:, :halo], power, length),
        "U": to_message(codes[:, halo:], power, length),
    }


def send(plan, slot, message_refs, messages):
    for step, ref in enumerate(message_refs):
        value = messages[plan[0][step]]
        for group in range(1, len(plan)):
            value = jnp.where(slot == group + 1, messages[plan[group][step]], value)
        ref[...] = value


def receive(plan, slot, message_refs, kind):
    value = message_refs[plan[0].index(kind)][...]
    for group in range(1, len(plan)):
        value = jnp.where(slot == group + 1, message_refs[plan[group].index(kind)][...], value)
    return value


def receive_halos(plan, slot, message_refs, rows):
    return jnp.concatenate(
        [from_message(receive(plan, slot, message_refs, kind), rows, 1) for kind in "UD"], axis=1
    )


def pack_kernel(quarter, features, *refs):
    steps = len(plan0[0])
    count = (len(refs) - steps - 6) // 2
    held_hbm, rows_hbm, *others_hbm = refs[: count + 2]
    *messages, held_ref, rows_ref = refs[count + 2 : count + steps + 4]
    others, (pick_ref, sems) = refs[count + steps + 4 : -2], refs[-2:]
    copies = [
        pltpu.make_async_copy(held_hbm, held_ref.at[pl.ds(0, held_hbm.shape[0])], sems.at[0]),
        pltpu.make_async_copy(rows_hbm, rows_ref, sems.at[1]),
    ]
    for index, (source, target) in enumerate(zip(others_hbm, others)):
        copies.append(pltpu.make_async_copy(source, target, sems.at[index + 2]))
    for copy in copies:
        copy.start()
    slot = slot_of(quarter)
    cells = pick_ref.shape[0]
    rows, halo, length = held_ref.shape[0] * 128 // cells, rows_ref.shape[1], messages[0].shape[0]
    held_ref[held_hbm.shape[0] :, :] = jnp.zeros(
        (held_ref.shape[0] - held_hbm.shape[0], 128), f32
    )
    copies[1].wait()
    cell = lax.broadcasted_iota(jnp.int32, (cells, halo), 0)
    for side in range(2):
        pick_ref[:, side * halo : (side + 1) * halo] = (
            cell == rows_ref[side : side + 1, :]
        ).astype(bf16)
    copies[0].wait()
    levels = features // 3

    @pl.when(slot == 0)
    def _():
        for group, kinds in enumerate(plan0):
            heat = load_rows(held_ref, group * levels, levels, cells)
            power = power_of(heat)
            messages[kinds.index("H")][...] = to_message(
                coded(heat, power), power, length
            )

    @pl.when(slot != 0)
    def _():
        state = load_rows(held_ref, 0, rows, cells)
        power = power_of(state)
        power = jnp.broadcast_to(jnp.max(power[:1], axis=1, keepdims=True), power.shape)
        high, low = split(state)
        sent = dot(high, pick_ref[...]) + dot(low, pick_ref[...])
        both = halo_messages(coded(sent, power), power, length)
        send(plan0, slot, messages, {**both, "H": both["U"]})

    for copy in copies[2:]:
        copy.wait()


def silu(v):
    half = 0.5 * v
    return half + half * jnp.tanh(half)


def network(state, w_in_ref, b_in_ref, w_mid_ref, b_mid_ref, w_out_ref, b_out_ref):
    def bias(ref):
        return jnp.concatenate([ref[...]] * (state.shape[1] // ref.shape[1]), axis=1)

    first = silu(dot(w_in_ref[...], state) + bias(b_in_ref)).astype(bf16)
    second = silu(dot(w_mid_ref[...], first) + bias(b_mid_ref)).astype(bf16)
    return dot(w_out_ref[...], second) + bias(b_out_ref)


def first_kernel(
    quarter, w_in_t_hbm, w_mid_hbm, w_out_hbm,
    held_ref, near_ref, diff_ref, tran_ref, b_in_ref, b_mid_ref, b_out_ref,
    matrix_ref, matrix_low_ref, keep_ref, part_ref, w_in_ref, c_in_ref, c_mid_ref, c_out_ref,
    w_mid_ref, w_out_ref, w_in_t_ref, sems,
):
    slot = slot_of(quarter)

    @pl.when(slot != 0)
    def _():
        sources = (w_in_t_hbm, w_mid_hbm, w_out_hbm)
        copies = [
            pltpu.make_async_copy(source, target, sems.at[index])
            for index, (source, target) in enumerate(zip(sources, (w_in_t_ref, w_mid_ref, w_out_ref)))
        ]
        for copy in copies:
            copy.start()
        rows, cells = part_ref.shape
        half_tran = 0.5 * tran_ref[...]
        weight = diff_ref[...] - half_tran
        keep = 1.0 - jnp.sum(diff_ref[...] + half_tran, axis=0, keepdims=True)
        keep_ref[...] = keep
        piece = 128
        for start in range(0, matrix_ref.shape[0], piece):
            cell = lax.broadcasted_iota(jnp.int32, (piece, cells), 0) + start
            total = jnp.zeros((piece, cells), f32)
            for edge in range(near_ref.shape[0]):
                total = total + jnp.where(
                    cell == near_ref[edge : edge + 1, :], weight[edge : edge + 1, :], 0.0
                )
            matrix_ref[start : start + piece, :], matrix_low_ref[start : start + piece, :] = split(total)
        state = load_rows(held_ref, 0, rows, cells)
        high, low = split(state)
        part_ref[...] = (
            dot(high, matrix_ref[:cells, :])
            + dot(high, matrix_low_ref[:cells, :])
            + dot(low, matrix_ref[:cells, :])
            + state * keep
        )
        for copy in copies:
            copy.wait()
        features = w_in_t_ref.shape[0]
        w_in_ref[...] = jnp.zeros_like(w_in_ref)
        w_in_ref[:, :features] = w_in_t_ref[...].T
        for row_ref, column_ref in ((b_in_ref, c_in_ref), (b_mid_ref, c_mid_ref), (b_out_ref, c_out_ref)):
            column_ref[...] = jnp.broadcast_to(row_ref[...], (128, row_ref.shape[1])).T


def middle_kernel(
    quarter, received, pick_ref, part_ref, matrix_ref, matrix_low_ref,
    w_in_ref, b_in_ref, w_mid_ref, b_mid_ref, w_out_ref, b_out_ref,
    messages, state_ref,
):
    slot = slot_of(quarter)
    @pl.when(slot != 0)
    def _():
        rows, cells = state_ref.shape
        levels, length = w_out_ref.shape[0], messages[0].shape[0]
        heat = from_message(receive(plan0, slot, received, "H"), levels, cells // 128)
        high, low = split(receive_halos(plan0, slot, received, rows))
        state_ref[...] = (
            part_ref[...]
            + dot(high, matrix_ref[cells:, :])
            + dot(high, matrix_low_ref[cells:, :])
            + dot(low, matrix_ref[cells:, :])
        )
        state_ref[:levels, :] = state_ref[:levels, :] + heat_gain * heat
        state = state_ref[...].astype(bf16)
        sent = dot(state, pick_ref[...])
        power = power_of(sent)
        out = halo_messages(coded(sent, power), power, length)
        heat = network(state, w_in_ref, b_in_ref, w_mid_ref, b_mid_ref, w_out_ref, b_out_ref)
        power = power_of(heat)
        out["H"] = to_message(coded(heat, power), power, length)
        send(plan1, slot, messages, out)


def own_kernel(
    quarter, held_ref, state_ref, matrix_ref, keep_ref,
    w_in_ref, b_in_ref, w_mid_ref, b_mid_ref, w_out_ref, b_out_ref, part_ref,
):
    slot = slot_of(quarter)

    @pl.when(slot != 0)
    def _():
        rows, cells = state_ref.shape
        levels = w_out_ref.shape[0]
        start = load_rows(held_ref, 0, rows, cells).astype(bf16)
        heat = network(start, w_in_ref, b_in_ref, w_mid_ref, b_mid_ref, w_out_ref, b_out_ref)
        state = state_ref[...]
        part_ref[...] = dot(state.astype(bf16), matrix_ref[:cells, :]) + state * keep_ref[...]
        part_ref[:levels, :] = part_ref[:levels, :] + heat_gain * heat


def last_kernel(quarter, received, part_ref, matrix_ref, out_ref):
    slot = slot_of(quarter)
    rows, cells = part_ref.shape
    tiles = cells // 128
    features = out_ref.shape[0] // tiles
    levels = features // 3

    def store_rows(first, values):
        for tile in range(tiles):
            out_ref[pl.ds(first * tiles + tile, values.shape[0], stride=tiles), :] = values[
                :, tile * 128 : (tile + 1) * 128
            ]

    @pl.when(slot == 0)
    def _():
        for group, kinds in enumerate(plan1):
            heat = from_message(received[kinds.index("H")][...], levels, tiles)
            store_rows(group * levels, heat)

    @pl.when(slot != 0)
    def _():
        halos = receive_halos(plan1, slot, received, rows).astype(bf16)
        store_rows(0, (part_ref[...] + dot(halos, matrix_ref[cells:, :]))[:features])


VMEM = pl.BlockSpec(memory_space=pltpu.VMEM)
HBM = pl.BlockSpec(memory_space=pltpu.HBM)


def call(kernel, name, out_shape, *args, hbm=0, scratch=(), flops=0, limit=16 << 20):
    size = sum(a.size * a.dtype.itemsize for a in args)
    args = [
        pltpu.with_memory_space_constraint(a, pltpu.HBM) if index < hbm else a
        for index, a in enumerate(args)
    ]
    return pl.pallas_call(
        kernel,
        out_shape=out_shape,
        in_specs=[HBM] * hbm + [VMEM] * (len(args) - hbm),
        out_specs=jax.tree.map(lambda _: VMEM, out_shape),
        scratch_shapes=scratch,
        compiler_params=pltpu.CompilerParams(vmem_limit_bytes=limit),
        cost_estimate=pl.CostEstimate(flops=flops, bytes_accessed=size, transcendentals=0),
        name=name,
    )(*args)


def exchange(plan, messages, quarter, blocks):
    def partner(group, block, step):
        slot, place = group // quarter, group % quarter
        kinds = [kinds[step] for kinds in plan]
        if slot == 0:
            return (kinds.index("H") + 1) * quarter + place, block
        kind = kinds[slot - 1]
        if kind == "H":
            return place, block
        return group, (block + (1 if kind == "U" else -1)) % blocks

    received = []
    for step, message in enumerate(messages):
        pairs = []
        for group in range(4 * quarter):
            for block in range(blocks):
                to_group, to_block = partner(group, block, step)
                pairs.append((group * blocks + block, to_group * blocks + to_block))
        received.append(lax.ppermute(message, ("grp", "blk"), pairs))
    return received


def body(held, neighbours, send_rows, diffusion, transport, w_in, b_in, w_mid, b_mid, w_out, b_out):
    quarter, blocks = lax.axis_size("grp") // 4, lax.axis_size("blk")
    _, fields, levels, cells = held.shape
    halo, hidden = send_rows.shape[1], w_mid.shape[0]
    features, tiles = fields * levels, cells // 128
    rows = -(-features // 16) * 16
    length = -(-(max(levels * tiles, rows) + 8) // 16) * 16

    def shape(*dims, dtype=f32):
        return jax.ShapeDtypeStruct(dims, dtype)

    def like(array):
        return shape(*array.shape, dtype=array.dtype)

    message = shape(length, 128, dtype=i16)
    full = shape(rows, cells)
    matrix_shape = shape(cells + 2 * halo, cells, dtype=bf16)
    count0, count1 = len(plan0[0]), len(plan1[0])
    args = (neighbours, diffusion, transport, b_in[None], b_mid[None], b_out[None])
    *messages, flat, _, near, diff, tran, b_in, b_mid, b_out, pick = call(
        lambda *refs: pack_kernel(quarter, features, *refs), "pack",
        [message] * len(plan0[0])
        + [shape(rows * tiles, 128), like(send_rows)]
        + [like(array) for array in args]
        + [shape(cells, 2 * halo, dtype=bf16)],
        held.reshape(features * tiles, 128), send_rows, *args,
        hbm=2 + len(args), scratch=[pltpu.SemaphoreType.DMA((2 + len(args),))],
    )
    received = exchange(plan0, messages, quarter, blocks)
    matrix, matrix_low, keep, part1, w_in, c_in, c_mid, c_out, w_mid, w_out = call(
        lambda *refs: first_kernel(quarter, *refs), "first",
        [
            matrix_shape, matrix_shape, shape(1, cells), full,
            shape(hidden, rows, dtype=bf16), shape(hidden, 128), shape(hidden, 128), shape(levels, 128),
            like(w_mid), like(w_out),
        ],
        w_in.T, w_mid, w_out, flat, near, diff, tran, b_in, b_mid, b_out,
        hbm=3, scratch=[pltpu.VMEM((features, hidden), bf16), pltpu.SemaphoreType.DMA((3,))],
        flops=2 * cells * hidden * hidden,
    )
    weights = (w_in, c_in, w_mid, c_mid, w_out, c_out)
    *messages, state1 = call(
        lambda *refs: middle_kernel(
            quarter, refs[:count0], *refs[count0 : count0 + 10], refs[count0 + 10 : -1], refs[-1]
        ),
        "middle", [message] * count1 + [full],
        *received, pick, part1, matrix, matrix_low, *weights, flops=2 * cells * hidden * hidden,
    )
    received = exchange(plan1, messages, quarter, blocks)
    part2 = call(
        lambda *refs: own_kernel(quarter, *refs), "own", full, flat, state1, matrix, keep, *weights, flops=2 * cells * hidden * hidden
    )
    out = call(
        lambda *refs: last_kernel(quarter, refs[:count1], *refs[count1:]), "last",
        shape(features * tiles, 128), *received, part2, matrix, flops=2 * rows * cells * 2 * halo,
    )
    return out.reshape(held.shape)


def solution(mesh):
    placed = (
        P("grp", None, None, "blk"),
        P(None, "blk"),
        P(None, "blk"),
        P(None, "blk"),
        P(None, "blk"),
        P(),
        P(),
        P(),
        P(),
        P(),
        P(),
    )
    return jax.shard_map(
        body, mesh=mesh, in_specs=placed, out_specs=P("grp", None, None, "blk"), check_vma=False
    )
```

```python
import functools
import math

import jax
import jax.numpy as jnp
from jax import lax
from jax.experimental import pallas as pl
from jax.experimental.pallas import tpu as pltpu
from jax.sharding import PartitionSpec as P

heat_gain = 0.5
bf16, f32, i16 = jnp.bfloat16, jnp.float32, jnp.int16

plan0 = ("UDH", "UHD", "HUD")
plan1 = ("UDH", "UHD", "HUD")


def dot(a, b):
    return jnp.dot(a, b, preferred_element_type=f32)


def split(values):
    high = values.astype(bf16)
    return high, (values - high.astype(f32)).astype(bf16)


def slot_of(quarter):
    return lax.axis_index("grp") // quarter


def load_rows(ref, first, rows, cells):
    tiles = cells // 128
    return jnp.concatenate(
        [ref[pl.ds(first * tiles + tile, rows, stride=tiles), :] for tile in range(tiles)], axis=1
    )


def power_of(values):
    largest = jnp.max(jnp.abs(values), axis=0, keepdims=True)
    largest = functools.reduce(
        jnp.maximum, [largest[:, at : at + 128] for at in range(0, values.shape[1], 128)]
    )
    power = jnp.ceil(jnp.log(jnp.maximum(largest, 1e-30) * (1 / 32000)) * (8 / math.log(2)))
    return jnp.broadcast_to(power, (8, 128))


def coded(values, power):
    factor = jnp.exp2(power[:1] * (-1 / 8))
    return jnp.round(values * jnp.concatenate([factor] * (values.shape[1] // 128), axis=1))


def to_message(codes, power, length):
    tiles = [codes[:, at : at + 128] for at in range(0, codes.shape[1], 128)]
    spare = length - power.shape[0] - len(tiles) * codes.shape[0]
    if spare:
        tiles.append(jnp.zeros((spare, 128), f32))
    return jnp.concatenate([*tiles, power], axis=0).astype(jnp.int32).astype(i16)


def from_message(message, rows, tiles):
    values = message.astype(f32)
    values = values[: rows * tiles] * jnp.exp2(values[-1:] * (1 / 8))
    return jnp.concatenate([values[at * rows : (at + 1) * rows] for at in range(tiles)], axis=1)


def halo_messages(codes, power, length):
    halo = codes.shape[1] // 2
    return {
        "D": to_message(codes[:, :halo], power, length),
        "U": to_message(codes[:, halo:], power, length),
    }


def send(plan, slot, message_refs, messages):
    for step, ref in enumerate(message_refs):
        value = messages[plan[0][step]]
        for group in range(1, len(plan)):
            value = jnp.where(slot == group + 1, messages[plan[group][step]], value)
        ref[...] = value


def receive(plan, slot, message_refs, kind):
    value = message_refs[plan[0].index(kind)][...]
    for group in range(1, len(plan)):
        value = jnp.where(slot == group + 1, message_refs[plan[group].index(kind)][...], value)
    return value


def receive_halos(plan, slot, message_refs, rows):
    return jnp.concatenate(
        [from_message(receive(plan, slot, message_refs, kind), rows, 1) for kind in "UD"], axis=1
    )


def pack_kernel(quarter, features, *refs):
    steps = len(plan0[0])
    count = (len(refs) - steps - 6) // 2
    held_hbm, rows_hbm, *others_hbm = refs[: count + 2]
    *messages, held_ref, rows_ref = refs[count + 2 : count + steps + 4]
    others, (pick_ref, sems) = refs[count + steps + 4 : -2], refs[-2:]
    copies = [
        pltpu.make_async_copy(held_hbm, held_ref.at[pl.ds(0, held_hbm.shape[0])], sems.at[0]),
        pltpu.make_async_copy(rows_hbm, rows_ref, sems.at[1]),
    ]
    for index, (source, target) in enumerate(zip(others_hbm, others)):
        copies.append(pltpu.make_async_copy(source, target, sems.at[index + 2]))
    for copy in copies:
        copy.start()
    slot = slot_of(quarter)
    cells = pick_ref.shape[0]
    rows, halo, length = held_ref.shape[0] * 128 // cells, rows_ref.shape[1], messages[0].shape[0]
    held_ref[held_hbm.shape[0] :, :] = jnp.zeros(
        (held_ref.shape[0] - held_hbm.shape[0], 128), f32
    )
    copies[1].wait()
    cell = lax.broadcasted_iota(jnp.int32, (cells, halo), 0)
    for side in range(2):
        pick_ref[:, side * halo : (side + 1) * halo] = (
            cell == rows_ref[side : side + 1, :]
        ).astype(bf16)
    copies[0].wait()
    levels = features // 3

    @pl.when(slot == 0)
    def _():
        for group, kinds in enumerate(plan0):
            heat = load_rows(held_ref, group * levels, levels, cells)
            power = power_of(heat)
            messages[kinds.index("H")][...] = to_message(
                coded(heat, power), power, length
            )

    @pl.when(slot != 0)
    def _():
        state = load_rows(held_ref, 0, rows, cells)
        high, low = split(state)
        sent = dot(high, pick_ref[...]) + dot(low, pick_ref[...])
        power = power_of(sent)
        both = halo_messages(coded(sent, power), power, length)
        send(plan0, slot, messages, {**both, "H": both["U"]})

    for copy in copies[2:]:
        copy.wait()


def silu(v):
    half = 0.5 * v
    return half + half * jnp.tanh(half)


def network(state, w_in_ref, b_in_ref, w_mid_ref, b_mid_ref, w_out_ref, b_out_ref):
    def bias(ref):
        return jnp.concatenate([ref[...]] * (state.shape[1] // ref.shape[1]), axis=1)

    first = silu(dot(w_in_ref[...], state) + bias(b_in_ref)).astype(bf16)
    second = silu(dot(w_mid_ref[...], first) + bias(b_mid_ref)).astype(bf16)
    return dot(w_out_ref[...], second) + bias(b_out_ref)


def first_kernel(
    quarter, w_in_t_hbm, w_mid_hbm, w_out_hbm,
    held_ref, near_ref, diff_ref, tran_ref, b_in_ref, b_mid_ref, b_out_ref,
    matrix_ref, matrix_low_ref, halo_matrix_ref, keep_ref, part_ref, w_in_ref, c_in_ref, c_mid_ref, c_out_ref,
    w_mid_ref, w_out_ref, w_in_t_ref, sems,
):
    slot = slot_of(quarter)

    @pl.when(slot != 0)
    def _():
        sources = (w_in_t_hbm, w_mid_hbm, w_out_hbm)
        copies = [
            pltpu.make_async_copy(source, target, sems.at[index])
            for index, (source, target) in enumerate(zip(sources, (w_in_t_ref, w_mid_ref, w_out_ref)))
        ]
        for copy in copies:
            copy.start()
        rows, cells = part_ref.shape
        half_tran = 0.5 * tran_ref[...]
        weight = diff_ref[...] - half_tran
        keep = 1.0 - jnp.sum(diff_ref[...] + half_tran, axis=0, keepdims=True)
        keep_ref[...] = keep
        piece = 128
        for start in range(0, matrix_ref.shape[0], piece):
            cell = lax.broadcasted_iota(jnp.int32, (piece, cells), 0) + start
            total = jnp.zeros((piece, cells), f32)
            for edge in range(near_ref.shape[0]):
                total = total + jnp.where(
                    cell == near_ref[edge : edge + 1, :], weight[edge : edge + 1, :], 0.0
                )
            high, low = split(total)
            matrix_ref[start : start + piece, :] = high
            if start < cells:
                matrix_low_ref[start : start + piece, :] = low
            else:
                size = matrix_ref.shape[0] - cells
                for at, half in enumerate((high, high, low)):
                    place = at * size + start - cells
                    halo_matrix_ref[place : place + piece, :] = half
        state = load_rows(held_ref, 0, rows, cells)
        high, low = split(state)
        part_ref[...] = (
            dot(high, matrix_ref[:cells, :])
            + dot(high, matrix_low_ref[...])
            + dot(low, matrix_ref[:cells, :])
            + state * keep
        )
        for copy in copies:
            copy.wait()
        features = w_in_t_ref.shape[0]
        w_in_ref[...] = jnp.zeros_like(w_in_ref)
        w_in_ref[:, :features] = w_in_t_ref[...].T
        for row_ref, column_ref in ((b_in_ref, c_in_ref), (b_mid_ref, c_mid_ref), (b_out_ref, c_out_ref)):
            column_ref[...] = jnp.broadcast_to(row_ref[...], (128, row_ref.shape[1])).T


def middle_kernel(
    quarter, received, pick_ref, part_ref, halo_matrix_ref,
    w_in_ref, b_in_ref, w_mid_ref, b_mid_ref, w_out_ref, b_out_ref,
    messages, state_ref,
):
    slot = slot_of(quarter)
    @pl.when(slot != 0)
    def _():
        rows, cells = state_ref.shape
        levels, length = w_out_ref.shape[0], messages[0].shape[0]
        heat = from_message(receive(plan0, slot, received, "H"), levels, cells // 128)
        high, low = split(receive_halos(plan0, slot, received, rows))
        state_ref[...] = part_ref[...] + dot(
            jnp.concatenate([high, low, high], axis=1), halo_matrix_ref[...]
        )
        state_ref[:levels, :] = state_ref[:levels, :] + heat_gain * heat
        state = state_ref[...].astype(bf16)
        sent = dot(state, pick_ref[...])
        power = power_of(sent)
        out = halo_messages(coded(sent, power), power, length)
        heat = network(state, w_in_ref, b_in_ref, w_mid_ref, b_mid_ref, w_out_ref, b_out_ref)
        power = power_of(heat)
        out["H"] = to_message(coded(heat, power), power, length)
        send(plan1, slot, messages, out)


def own_kernel(
    quarter, held_ref, state_ref, matrix_ref, matrix_low_ref, keep_ref,
    w_in_ref, b_in_ref, w_mid_ref, b_mid_ref, w_out_ref, b_out_ref, part_ref,
):
    slot = slot_of(quarter)

    @pl.when(slot != 0)
    def _():
        rows, cells = state_ref.shape
        levels = w_out_ref.shape[0]
        start = load_rows(held_ref, 0, rows, cells).astype(bf16)
        heat = network(start, w_in_ref, b_in_ref, w_mid_ref, b_mid_ref, w_out_ref, b_out_ref)
        state = state_ref[...]
        high = state.astype(bf16)
        part_ref[...] = (
            dot(high, matrix_ref[:cells, :]) + dot(high, matrix_low_ref[...]) + state * keep_ref[...]
        )
        part_ref[:levels, :] = part_ref[:levels, :] + heat_gain * heat


def last_kernel(quarter, received, part_ref, matrix_ref, out_ref):
    slot = slot_of(quarter)
    rows, cells = part_ref.shape
    tiles = cells // 128
    features = out_ref.shape[0] // tiles
    levels = features // 3

    def store_rows(first, values):
        for tile in range(tiles):
            out_ref[pl.ds(first * tiles + tile, values.shape[0], stride=tiles), :] = values[
                :, tile * 128 : (tile + 1) * 128
            ]

    @pl.when(slot == 0)
    def _():
        for group, kinds in enumerate(plan1):
            heat = from_message(received[kinds.index("H")][...], levels, tiles)
            store_rows(group * levels, heat)

    @pl.when(slot != 0)
    def _():
        halos = receive_halos(plan1, slot, received, rows).astype(bf16)
        store_rows(0, (part_ref[...] + dot(halos, matrix_ref[cells:, :]))[:features])


VMEM = pl.BlockSpec(memory_space=pltpu.VMEM)
HBM = pl.BlockSpec(memory_space=pltpu.HBM)


def call(kernel, name, out_shape, *args, hbm=0, scratch=(), flops=0, limit=16 << 20):
    size = sum(a.size * a.dtype.itemsize for a in args)
    args = [
        pltpu.with_memory_space_constraint(a, pltpu.HBM) if index < hbm else a
        for index, a in enumerate(args)
    ]
    return pl.pallas_call(
        kernel,
        out_shape=out_shape,
        in_specs=[HBM] * hbm + [VMEM] * (len(args) - hbm),
        out_specs=jax.tree.map(lambda _: VMEM, out_shape),
        scratch_shapes=scratch,
        compiler_params=pltpu.CompilerParams(vmem_limit_bytes=limit),
        cost_estimate=pl.CostEstimate(flops=flops, bytes_accessed=size, transcendentals=0),
        name=name,
    )(*args)


def exchange(plan, messages, quarter, blocks):
    def partner(group, block, step):
        slot, place = group // quarter, group % quarter
        kinds = [kinds[step] for kinds in plan]
        if slot == 0:
            return (kinds.index("H") + 1) * quarter + place, block
        kind = kinds[slot - 1]
        if kind == "H":
            return place, block
        return group, (block + (1 if kind == "U" else -1)) % blocks

    received = []
    for step, message in enumerate(messages):
        pairs = []
        for group in range(4 * quarter):
            for block in range(blocks):
                to_group, to_block = partner(group, block, step)
                pairs.append((group * blocks + block, to_group * blocks + to_block))
        received.append(lax.ppermute(message, ("grp", "blk"), pairs))
    return received


def body(held, neighbours, send_rows, diffusion, transport, w_in, b_in, w_mid, b_mid, w_out, b_out):
    quarter, blocks = lax.axis_size("grp") // 4, lax.axis_size("blk")
    _, fields, levels, cells = held.shape
    halo, hidden = send_rows.shape[1], w_mid.shape[0]
    features, tiles = fields * levels, cells // 128
    rows = -(-features // 16) * 16
    length = -(-(max(levels * tiles, rows) + 8) // 16) * 16

    def shape(*dims, dtype=f32):
        return jax.ShapeDtypeStruct(dims, dtype)

    def like(array):
        return shape(*array.shape, dtype=array.dtype)

    message = shape(length, 128, dtype=i16)
    full = shape(rows, cells)
    matrix_shape = shape(cells + 2 * halo, cells, dtype=bf16)
    count0, count1 = len(plan0[0]), len(plan1[0])
    args = (neighbours, diffusion, transport, b_in[None], b_mid[None], b_out[None])
    *messages, flat, _, near, diff, tran, b_in, b_mid, b_out, pick = call(
        lambda *refs: pack_kernel(quarter, features, *refs), "pack",
        [message] * len(plan0[0])
        + [shape(rows * tiles, 128), like(send_rows)]
        + [like(array) for array in args]
        + [shape(cells, 2 * halo, dtype=bf16)],
        held.reshape(features * tiles, 128), send_rows, *args,
        hbm=2 + len(args), scratch=[pltpu.SemaphoreType.DMA((2 + len(args),))],
    )
    received = exchange(plan0, messages, quarter, blocks)
    matrix, matrix_low, halo_matrix, keep, part1, w_in, c_in, c_mid, c_out, w_mid, w_out = call(
        lambda *refs: first_kernel(quarter, *refs), "first",
        [
            matrix_shape, shape(cells, cells, dtype=bf16), shape(6 * halo, cells, dtype=bf16),
            shape(1, cells), full,
            shape(hidden, rows, dtype=bf16), shape(hidden, 128), shape(hidden, 128), shape(levels, 128),
            like(w_mid), like(w_out),
        ],
        w_in.T, w_mid, w_out, flat, near, diff, tran, b_in, b_mid, b_out,
        hbm=3, scratch=[pltpu.VMEM((features, hidden), bf16), pltpu.SemaphoreType.DMA((3,))],
        flops=2 * cells * hidden * hidden,
    )
    weights = (w_in, c_in, w_mid, c_mid, w_out, c_out)
    *messages, state1 = call(
        lambda *refs: middle_kernel(
            quarter, refs[:count0], *refs[count0 : count0 + 9], refs[count0 + 9 : -1], refs[-1]
        ),
        "middle", [message] * count1 + [full],
        *received, pick, part1, halo_matrix, *weights, flops=2 * cells * hidden * hidden,
    )
    received = exchange(plan1, messages, quarter, blocks)
    part2 = call(
        lambda *refs: own_kernel(quarter, *refs), "own", full, flat, state1, matrix, matrix_low, keep, *weights, flops=2 * cells * hidden * hidden
    )
    out = call(
        lambda *refs: last_kernel(quarter, refs[:count1], *refs[count1:]), "last",
        shape(features * tiles, 128), *received, part2, matrix, flops=2 * rows * cells * 2 * halo,
    )
    return out.reshape(held.shape)


def solution(mesh):
    placed = (
        P("grp", None, None, "blk"),
        P(None, "blk"),
        P(None, "blk"),
        P(None, "blk"),
        P(None, "blk"),
        P(),
        P(),
        P(),
        P(),
        P(),
        P(),
    )
    return jax.shard_map(
        body, mesh=mesh, in_specs=placed, out_specs=P("grp", None, None, "blk"), check_vma=False
    )
```

```python
import functools
import math

import jax
import jax.numpy as jnp
from jax import lax
from jax.experimental import pallas as pl
from jax.experimental.pallas import tpu as pltpu
from jax.sharding import PartitionSpec as P

heat_gain = 0.5
bf16, f32, i16 = jnp.bfloat16, jnp.float32, jnp.int16

plan0 = ("UDH", "UHD", "HUD")
plan1 = ("UDH", "UHD", "HUD")


def dot(a, b):
    return jnp.dot(a, b, preferred_element_type=f32)


def split(values):
    high = values.astype(bf16)
    return high, (values - high.astype(f32)).astype(bf16)


def slot_of(quarter):
    return lax.axis_index("grp") // quarter


def load_rows(ref, first, rows, cells):
    tiles = cells // 128
    return jnp.concatenate(
        [ref[pl.ds(first * tiles + tile, rows, stride=tiles), :] for tile in range(tiles)], axis=1
    )


def power_of(values):
    largest = jnp.max(jnp.abs(values), axis=0, keepdims=True)
    largest = functools.reduce(
        jnp.maximum, [largest[:, at : at + 128] for at in range(0, values.shape[1], 128)]
    )
    power = jnp.ceil(jnp.log(jnp.maximum(largest, 1e-30) * (1 / 32000)) * (8 / math.log(2)))
    return jnp.broadcast_to(power, (8, 128))


def coded(values, power):
    factor = jnp.exp2(power[:1] * (-1 / 8))
    return jnp.round(values * jnp.concatenate([factor] * (values.shape[1] // 128), axis=1))


def to_message(codes, power, length):
    tiles = [codes[:, at : at + 128] for at in range(0, codes.shape[1], 128)]
    spare = length - power.shape[0] - len(tiles) * codes.shape[0]
    if spare:
        tiles.append(jnp.zeros((spare, 128), f32))
    return jnp.concatenate([*tiles, power], axis=0).astype(jnp.int32).astype(i16)


def from_message(message, rows, tiles):
    values = message.astype(f32)
    values = values[: rows * tiles] * jnp.exp2(values[-1:] * (1 / 8))
    return jnp.concatenate([values[at * rows : (at + 1) * rows] for at in range(tiles)], axis=1)


def halo_messages(codes, power, length):
    halo = codes.shape[1] // 2
    return {
        "D": to_message(codes[:, :halo], power, length),
        "U": to_message(codes[:, halo:], power, length),
    }


def send(plan, slot, message_refs, messages):
    for step, ref in enumerate(message_refs):
        value = messages[plan[0][step]]
        for group in range(1, len(plan)):
            value = jnp.where(slot == group + 1, messages[plan[group][step]], value)
        ref[...] = value


def receive(plan, slot, message_refs, kind):
    value = message_refs[plan[0].index(kind)][...]
    for group in range(1, len(plan)):
        value = jnp.where(slot == group + 1, message_refs[plan[group].index(kind)][...], value)
    return value


def receive_halos(plan, slot, message_refs, rows):
    return jnp.concatenate(
        [from_message(receive(plan, slot, message_refs, kind), rows, 1) for kind in "UD"], axis=1
    )


def pack_kernel(quarter, features, *refs):
    steps = len(plan0[0])
    count = (len(refs) - steps - 6) // 2
    held_hbm, rows_hbm, *others_hbm = refs[: count + 2]
    *messages, held_ref, rows_ref = refs[count + 2 : count + steps + 4]
    others, (pick_ref, sems) = refs[count + steps + 4 : -2], refs[-2:]
    copies = [
        pltpu.make_async_copy(held_hbm, held_ref.at[pl.ds(0, held_hbm.shape[0])], sems.at[0]),
        pltpu.make_async_copy(rows_hbm, rows_ref, sems.at[1]),
    ]
    for index, (source, target) in enumerate(zip(others_hbm, others)):
        copies.append(pltpu.make_async_copy(source, target, sems.at[index + 2]))
    for copy in copies:
        copy.start()
    slot = slot_of(quarter)
    cells = pick_ref.shape[0]
    rows, halo, length = held_ref.shape[0] * 128 // cells, rows_ref.shape[1], messages[0].shape[0]
    held_ref[held_hbm.shape[0] :, :] = jnp.zeros(
        (held_ref.shape[0] - held_hbm.shape[0], 128), f32
    )
    copies[1].wait()
    cell = lax.broadcasted_iota(jnp.int32, (cells, halo), 0)
    for side in range(2):
        pick_ref[:, side * halo : (side + 1) * halo] = (
            cell == rows_ref[side : side + 1, :]
        ).astype(bf16)
    copies[0].wait()
    levels = features // 3

    @pl.when(slot == 0)
    def _():
        for group, kinds in enumerate(plan0):
            heat = load_rows(held_ref, group * levels, levels, cells)
            power = power_of(heat)
            messages[kinds.index("H")][...] = to_message(
                coded(heat, power), power, length
            )

    @pl.when(slot != 0)
    def _():
        state = load_rows(held_ref, 0, rows, cells)
        high, low = split(state)
        sent = dot(high, pick_ref[...]) + dot(low, pick_ref[...])
        power = power_of(sent)
        both = halo_messages(coded(sent, power), power, length)
        send(plan0, slot, messages, {**both, "H": both["U"]})

    for copy in copies[2:]:
        copy.wait()


def silu(half):
    return half + half * jnp.tanh(half)


def network(state, w_in_ref, b_in_ref, w_mid_ref, b_mid_ref, w_out_ref, b_out_ref):
    def bias(ref):
        return jnp.concatenate([ref[...]] * (state.shape[1] // ref.shape[1]), axis=1)

    first = silu(dot(w_in_ref[...], state) + bias(b_in_ref)).astype(bf16)
    second = silu(dot(w_mid_ref[...], first) + bias(b_mid_ref)).astype(bf16)
    return dot(w_out_ref[...], second) + bias(b_out_ref)


def first_kernel(
    quarter, w_in_t_hbm, w_mid_hbm, w_out_hbm,
    held_ref, near_ref, diff_ref, tran_ref, b_in_ref, b_mid_ref, b_out_ref,
    matrix_ref, matrix_low_ref, keep_ref, part_ref, w_in_ref, c_in_ref, c_mid_ref, c_out_ref,
    w_mid_ref, w_out_ref, w_in_t_ref, sems,
):
    slot = slot_of(quarter)

    @pl.when(slot != 0)
    def _():
        sources = (w_in_t_hbm, w_mid_hbm, w_out_hbm)
        copies = [
            pltpu.make_async_copy(source, target, sems.at[index])
            for index, (source, target) in enumerate(zip(sources, (w_in_t_ref, w_mid_ref, w_out_ref)))
        ]
        for copy in copies:
            copy.start()
        rows, cells = part_ref.shape
        half_tran = 0.5 * tran_ref[...]
        weight = diff_ref[...] - half_tran
        keep = 1.0 - jnp.sum(diff_ref[...] + half_tran, axis=0, keepdims=True)
        keep_ref[...] = keep
        piece = 128
        for start in range(0, matrix_ref.shape[0], piece):
            cell = lax.broadcasted_iota(jnp.int32, (piece, cells), 0) + start
            total = jnp.zeros((piece, cells), f32)
            for edge in range(near_ref.shape[0]):
                total = total + jnp.where(
                    cell == near_ref[edge : edge + 1, :], weight[edge : edge + 1, :], 0.0
                )
            matrix_ref[start : start + piece, :], matrix_low_ref[start : start + piece, :] = split(total)
        state = load_rows(held_ref, 0, rows, cells)
        high, low = split(state)
        part_ref[...] = (
            dot(high, matrix_ref[:cells, :])
            + dot(high, matrix_low_ref[:cells, :])
            + dot(low, matrix_ref[:cells, :])
            + state * keep
        )
        for copy in copies:
            copy.wait()
        features = w_in_t_ref.shape[0]
        w_in_ref[...] = jnp.zeros_like(w_in_ref)
        w_in_ref[:, :features] = (w_in_t_ref[...] * 0.5).T
        w_mid_ref[...] = w_mid_ref[...] * 0.5
        for row_ref, column_ref, part in (
            (b_in_ref, c_in_ref, 0.5), (b_mid_ref, c_mid_ref, 0.5), (b_out_ref, c_out_ref, 1.0),
        ):
            column_ref[...] = jnp.broadcast_to(row_ref[...] * part, (128, row_ref.shape[1])).T


def middle_kernel(
    quarter, received, pick_ref, part_ref, matrix_ref, matrix_low_ref,
    w_in_ref, b_in_ref, w_mid_ref, b_mid_ref, w_out_ref, b_out_ref,
    messages, state_ref,
):
    slot = slot_of(quarter)
    @pl.when(slot != 0)
    def _():
        rows, cells = state_ref.shape
        levels, length = w_out_ref.shape[0], messages[0].shape[0]
        heat = from_message(receive(plan0, slot, received, "H"), levels, cells // 128)
        high, low = split(receive_halos(plan0, slot, received, rows))
        state_ref[...] = (
            part_ref[...]
            + dot(high, matrix_ref[cells:, :])
            + dot(high, matrix_low_ref[cells:, :])
            + dot(low, matrix_ref[cells:, :])
        )
        state_ref[:levels, :] = state_ref[:levels, :] + heat_gain * heat
        state = state_ref[...].astype(bf16)
        sent = dot(state, pick_ref[...])
        power = power_of(sent)
        out = halo_messages(coded(sent, power), power, length)
        heat = network(state, w_in_ref, b_in_ref, w_mid_ref, b_mid_ref, w_out_ref, b_out_ref)
        power = power_of(heat)
        out["H"] = to_message(coded(heat, power), power, length)
        send(plan1, slot, messages, out)


def own_kernel(
    quarter, held_ref, state_ref, matrix_ref, keep_ref,
    w_in_ref, b_in_ref, w_mid_ref, b_mid_ref, w_out_ref, b_out_ref, part_ref,
):
    slot = slot_of(quarter)

    @pl.when(slot != 0)
    def _():
        rows, cells = state_ref.shape
        levels = w_out_ref.shape[0]
        start = load_rows(held_ref, 0, rows, cells).astype(bf16)
        heat = network(start, w_in_ref, b_in_ref, w_mid_ref, b_mid_ref, w_out_ref, b_out_ref)
        state = state_ref[...]
        part_ref[...] = dot(state.astype(bf16), matrix_ref[:cells, :]) + state * keep_ref[...]
        part_ref[:levels, :] = part_ref[:levels, :] + heat_gain * heat


def last_kernel(quarter, received, part_ref, matrix_ref, out_ref):
    slot = slot_of(quarter)
    rows, cells = part_ref.shape
    tiles = cells // 128
    features = out_ref.shape[0] // tiles
    levels = features // 3

    def store_rows(first, values):
        for tile in range(tiles):
            out_ref[pl.ds(first * tiles + tile, values.shape[0], stride=tiles), :] = values[
                :, tile * 128 : (tile + 1) * 128
            ]

    @pl.when(slot == 0)
    def _():
        for group, kinds in enumerate(plan1):
            heat = from_message(received[kinds.index("H")][...], levels, tiles)
            store_rows(group * levels, heat)

    @pl.when(slot != 0)
    def _():
        halos = receive_halos(plan1, slot, received, rows).astype(bf16)
        store_rows(0, (part_ref[...] + dot(halos, matrix_ref[cells:, :]))[:features])


VMEM = pl.BlockSpec(memory_space=pltpu.VMEM)
HBM = pl.BlockSpec(memory_space=pltpu.HBM)


def call(kernel, name, out_shape, *args, hbm=0, scratch=(), flops=0, limit=16 << 20):
    size = sum(a.size * a.dtype.itemsize for a in args)
    args = [
        pltpu.with_memory_space_constraint(a, pltpu.HBM) if index < hbm else a
        for index, a in enumerate(args)
    ]
    return pl.pallas_call(
        kernel,
        out_shape=out_shape,
        in_specs=[HBM] * hbm + [VMEM] * (len(args) - hbm),
        out_specs=jax.tree.map(lambda _: VMEM, out_shape),
        scratch_shapes=scratch,
        compiler_params=pltpu.CompilerParams(vmem_limit_bytes=limit),
        cost_estimate=pl.CostEstimate(flops=flops, bytes_accessed=size, transcendentals=0),
        name=name,
    )(*args)


def exchange(plan, messages, quarter, blocks):
    def partner(group, block, step):
        slot, place = group // quarter, group % quarter
        kinds = [kinds[step] for kinds in plan]
        if slot == 0:
            return (kinds.index("H") + 1) * quarter + place, block
        kind = kinds[slot - 1]
        if kind == "H":
            return place, block
        return group, (block + (1 if kind == "U" else -1)) % blocks

    received = []
    for step, message in enumerate(messages):
        pairs = []
        for group in range(4 * quarter):
            for block in range(blocks):
                to_group, to_block = partner(group, block, step)
                pairs.append((group * blocks + block, to_group * blocks + to_block))
        received.append(lax.ppermute(message, ("grp", "blk"), pairs))
    return received


def body(held, neighbours, send_rows, diffusion, transport, w_in, b_in, w_mid, b_mid, w_out, b_out):
    quarter, blocks = lax.axis_size("grp") // 4, lax.axis_size("blk")
    _, fields, levels, cells = held.shape
    halo, hidden = send_rows.shape[1], w_mid.shape[0]
    features, tiles = fields * levels, cells // 128
    rows = -(-features // 16) * 16
    length = -(-(max(levels * tiles, rows) + 8) // 16) * 16

    def shape(*dims, dtype=f32):
        return jax.ShapeDtypeStruct(dims, dtype)

    def like(array):
        return shape(*array.shape, dtype=array.dtype)

    message = shape(length, 128, dtype=i16)
    full = shape(rows, cells)
    matrix_shape = shape(cells + 2 * halo, cells, dtype=bf16)
    count0, count1 = len(plan0[0]), len(plan1[0])
    args = (neighbours, diffusion, transport, b_in[None], b_mid[None], b_out[None])
    *messages, flat, _, near, diff, tran, b_in, b_mid, b_out, pick = call(
        lambda *refs: pack_kernel(quarter, features, *refs), "pack",
        [message] * len(plan0[0])
        + [shape(rows * tiles, 128), like(send_rows)]
        + [like(array) for array in args]
        + [shape(cells, 2 * halo, dtype=bf16)],
        held.reshape(features * tiles, 128), send_rows, *args,
        hbm=2 + len(args), scratch=[pltpu.SemaphoreType.DMA((2 + len(args),))],
    )
    received = exchange(plan0, messages, quarter, blocks)
    matrix, matrix_low, keep, part1, w_in, c_in, c_mid, c_out, w_mid, w_out = call(
        lambda *refs: first_kernel(quarter, *refs), "first",
        [
            matrix_shape, matrix_shape, shape(1, cells), full,
            shape(hidden, rows, dtype=bf16), shape(hidden, 128), shape(hidden, 128), shape(levels, 128),
            like(w_mid), like(w_out),
        ],
        w_in.T, w_mid, w_out, flat, near, diff, tran, b_in, b_mid, b_out,
        hbm=3, scratch=[pltpu.VMEM((features, hidden), bf16), pltpu.SemaphoreType.DMA((3,))],
        flops=2 * cells * hidden * hidden,
    )
    weights = (w_in, c_in, w_mid, c_mid, w_out, c_out)
    *messages, state1 = call(
        lambda *refs: middle_kernel(
            quarter, refs[:count0], *refs[count0 : count0 + 10], refs[count0 + 10 : -1], refs[-1]
        ),
        "middle", [message] * count1 + [full],
        *received, pick, part1, matrix, matrix_low, *weights, flops=2 * cells * hidden * hidden,
    )
    received = exchange(plan1, messages, quarter, blocks)
    part2 = call(
        lambda *refs: own_kernel(quarter, *refs), "own", full, flat, state1, matrix, keep, *weights, flops=2 * cells * hidden * hidden
    )
    out = call(
        lambda *refs: last_kernel(quarter, refs[:count1], *refs[count1:]), "last",
        shape(features * tiles, 128), *received, part2, matrix, flops=2 * rows * cells * 2 * halo,
    )
    return out.reshape(held.shape)


def solution(mesh):
    placed = (
        P("grp", None, None, "blk"),
        P(None, "blk"),
        P(None, "blk"),
        P(None, "blk"),
        P(None, "blk"),
        P(),
        P(),
        P(),
        P(),
        P(),
        P(),
    )
    return jax.shard_map(
        body, mesh=mesh, in_specs=placed, out_specs=P("grp", None, None, "blk"), check_vma=False
    )
```

```python
import functools
import math

import jax
import jax.numpy as jnp
from jax import lax
from jax.experimental import pallas as pl
from jax.experimental.pallas import tpu as pltpu
from jax.sharding import PartitionSpec as P

heat_gain = 0.5
bf16, f32, i16 = jnp.bfloat16, jnp.float32, jnp.int16

plan0 = ("HUD", "UHD", "UDH")
plan1 = ("UDH", "UHD", "HUD")


def dot(a, b):
    return jnp.dot(a, b, preferred_element_type=f32)


def split(values):
    high = values.astype(bf16)
    return high, (values - high.astype(f32)).astype(bf16)


def slot_of(quarter):
    return lax.axis_index("grp") // quarter


def load_rows(ref, first, rows, cells):
    tiles = cells // 128
    return jnp.concatenate(
        [ref[pl.ds(first * tiles + tile, rows, stride=tiles), :] for tile in range(tiles)], axis=1
    )


def power_of(values):
    largest = jnp.max(jnp.abs(values), axis=0, keepdims=True)
    largest = functools.reduce(
        jnp.maximum, [largest[:, at : at + 128] for at in range(0, values.shape[1], 128)]
    )
    power = jnp.ceil(jnp.log(jnp.maximum(largest, 1e-30) * (1 / 32000)) * (8 / math.log(2)))
    return jnp.broadcast_to(power, (8, 128))


def coded(values, power):
    factor = jnp.exp2(power[:1] * (-1 / 8))
    return jnp.round(values * jnp.concatenate([factor] * (values.shape[1] // 128), axis=1))


def to_message(codes, power, length):
    tiles = [codes[:, at : at + 128] for at in range(0, codes.shape[1], 128)]
    spare = length - power.shape[0] - len(tiles) * codes.shape[0]
    if spare:
        tiles.append(jnp.zeros((spare, 128), f32))
    return jnp.concatenate([*tiles, power], axis=0).astype(jnp.int32).astype(i16)


def from_message(message, rows, tiles):
    values = message.astype(f32)
    values = values[: rows * tiles] * jnp.exp2(values[-1:] * (1 / 8))
    return jnp.concatenate([values[at * rows : (at + 1) * rows] for at in range(tiles)], axis=1)


def halo_messages(codes, power, length):
    halo = codes.shape[1] // 2
    return {
        "D": to_message(codes[:, :halo], power, length),
        "U": to_message(codes[:, halo:], power, length),
    }


def send(plan, slot, message_refs, messages):
    for step, ref in enumerate(message_refs):
        value = messages[plan[0][step]]
        for group in range(1, len(plan)):
            value = jnp.where(slot == group + 1, messages[plan[group][step]], value)
        ref[...] = value


def receive(plan, slot, message_refs, kind):
    value = message_refs[plan[0].index(kind)][...]
    for group in range(1, len(plan)):
        value = jnp.where(slot == group + 1, message_refs[plan[group].index(kind)][...], value)
    return value


def receive_halos(plan, slot, message_refs, rows):
    return jnp.concatenate(
        [from_message(receive(plan, slot, message_refs, kind), rows, 1) for kind in "UD"], axis=1
    )


def pack_kernel(quarter, features, *refs):
    steps = len(plan0[0])
    count = (len(refs) - steps - 6) // 2
    held_hbm, rows_hbm, *others_hbm = refs[: count + 2]
    *messages, held_ref, rows_ref = refs[count + 2 : count + steps + 4]
    others, (pick_ref, sems) = refs[count + steps + 4 : -2], refs[-2:]
    copies = [
        pltpu.make_async_copy(held_hbm, held_ref.at[pl.ds(0, held_hbm.shape[0])], sems.at[0]),
        pltpu.make_async_copy(rows_hbm, rows_ref, sems.at[1]),
    ]
    for index, (source, target) in enumerate(zip(others_hbm, others)):
        copies.append(pltpu.make_async_copy(source, target, sems.at[index + 2]))
    for copy in copies:
        copy.start()
    slot = slot_of(quarter)
    cells = pick_ref.shape[0]
    rows, halo, length = held_ref.shape[0] * 128 // cells, rows_ref.shape[1], messages[0].shape[0]
    held_ref[held_hbm.shape[0] :, :] = jnp.zeros(
        (held_ref.shape[0] - held_hbm.shape[0], 128), f32
    )
    copies[1].wait()
    cell = lax.broadcasted_iota(jnp.int32, (cells, halo), 0)
    for side in range(2):
        pick_ref[:, side * halo : (side + 1) * halo] = (
            cell == rows_ref[side : side + 1, :]
        ).astype(bf16)
    copies[0].wait()
    levels = features // 3

    @pl.when(slot == 0)
    def _():
        for group, kinds in enumerate(plan0):
            heat = load_rows(held_ref, group * levels, levels, cells)
            power = power_of(heat)
            messages[kinds.index("H")][...] = to_message(
                coded(heat, power), power, length
            )

    @pl.when(slot != 0)
    def _():
        state = load_rows(held_ref, 0, rows, cells)
        high, low = split(state)
        sent = dot(high, pick_ref[...]) + dot(low, pick_ref[...])
        power = power_of(sent)
        both = halo_messages(coded(sent, power), power, length)
        send(plan0, slot, messages, {**both, "H": both["U"]})

    for copy in copies[2:]:
        copy.wait()


def silu(v):
    half = 0.5 * v
    return half + half * jnp.tanh(half)


def network(state, w_in_ref, b_in_ref, w_mid_ref, b_mid_ref, w_out_ref, b_out_ref):
    def bias(ref):
        return jnp.concatenate([ref[...]] * (state.shape[1] // ref.shape[1]), axis=1)

    first = silu(dot(w_in_ref[...], state) + bias(b_in_ref)).astype(bf16)
    second = silu(dot(w_mid_ref[...], first) + bias(b_mid_ref)).astype(bf16)
    return dot(w_out_ref[...], second) + bias(b_out_ref)


def first_kernel(
    quarter, w_in_t_hbm, w_mid_hbm, w_out_hbm,
    held_ref, near_ref, diff_ref, tran_ref, b_in_ref, b_mid_ref, b_out_ref,
    matrix_ref, matrix_low_ref, keep_ref, part_ref, w_in_ref, c_in_ref, c_mid_ref, c_out_ref,
    w_mid_ref, w_out_ref, w_in_t_ref, sems,
):
    slot = slot_of(quarter)

    @pl.when(slot != 0)
    def _():
        sources = (w_in_t_hbm, w_mid_hbm, w_out_hbm)
        copies = [
            pltpu.make_async_copy(source, target, sems.at[index])
            for index, (source, target) in enumerate(zip(sources, (w_in_t_ref, w_mid_ref, w_out_ref)))
        ]
        for copy in copies:
            copy.start()
        rows, cells = part_ref.shape
        half_tran = 0.5 * tran_ref[...]
        weight = diff_ref[...] - half_tran
        keep = 1.0 - jnp.sum(diff_ref[...] + half_tran, axis=0, keepdims=True)
        keep_ref[...] = keep
        piece = 128
        for start in range(0, matrix_ref.shape[0], piece):
            cell = lax.broadcasted_iota(jnp.int32, (piece, cells), 0) + start
            total = jnp.zeros((piece, cells), f32)
            for edge in range(near_ref.shape[0]):
                total = total + jnp.where(
                    cell == near_ref[edge : edge + 1, :], weight[edge : edge + 1, :], 0.0
                )
            matrix_ref[start : start + piece, :], matrix_low_ref[start : start + piece, :] = split(total)
        state = load_rows(held_ref, 0, rows, cells)
        high, low = split(state)
        part_ref[...] = (
            dot(high, matrix_ref[:cells, :])
            + dot(high, matrix_low_ref[:cells, :])
            + dot(low, matrix_ref[:cells, :])
            + state * keep
        )
        for copy in copies:
            copy.wait()
        features = w_in_t_ref.shape[0]
        w_in_ref[...] = jnp.zeros_like(w_in_ref)
        w_in_ref[:, :features] = w_in_t_ref[...].T
        for row_ref, column_ref in ((b_in_ref, c_in_ref), (b_mid_ref, c_mid_ref), (b_out_ref, c_out_ref)):
            column_ref[...] = jnp.broadcast_to(row_ref[...], (128, row_ref.shape[1])).T


def middle_kernel(
    quarter, received, pick_ref, part_ref, matrix_ref, matrix_low_ref,
    w_in_ref, b_in_ref, w_mid_ref, b_mid_ref, w_out_ref, b_out_ref,
    messages, state_ref,
):
    slot = slot_of(quarter)
    @pl.when(slot != 0)
    def _():
        rows, cells = state_ref.shape
        levels, length = w_out_ref.shape[0], messages[0].shape[0]
        heat = from_message(receive(plan0, slot, received, "H"), levels, cells // 128)
        high, low = split(receive_halos(plan0, slot, received, rows))
        state_ref[...] = (
            part_ref[...]
            + dot(high, matrix_ref[cells:, :])
            + dot(high, matrix_low_ref[cells:, :])
            + dot(low, matrix_ref[cells:, :])
        )
        state_ref[:levels, :] = state_ref[:levels, :] + heat_gain * heat
        state = state_ref[...].astype(bf16)
        sent = dot(state, pick_ref[...])
        power = power_of(sent)
        out = halo_messages(coded(sent, power), power, length)
        heat = network(state, w_in_ref, b_in_ref, w_mid_ref, b_mid_ref, w_out_ref, b_out_ref)
        power = power_of(heat)
        out["H"] = to_message(coded(heat, power), power, length)
        send(plan1, slot, messages, out)


def own_kernel(
    quarter, held_ref, state_ref, matrix_ref, keep_ref,
    w_in_ref, b_in_ref, w_mid_ref, b_mid_ref, w_out_ref, b_out_ref, part_ref,
):
    slot = slot_of(quarter)

    @pl.when(slot != 0)
    def _():
        rows, cells = state_ref.shape
        levels = w_out_ref.shape[0]
        start = load_rows(held_ref, 0, rows, cells).astype(bf16)
        heat = network(start, w_in_ref, b_in_ref, w_mid_ref, b_mid_ref, w_out_ref, b_out_ref)
        state = state_ref[...]
        part_ref[...] = dot(state.astype(bf16), matrix_ref[:cells, :]) + state * keep_ref[...]
        part_ref[:levels, :] = part_ref[:levels, :] + heat_gain * heat


def last_kernel(quarter, received, part_ref, matrix_ref, out_ref):
    slot = slot_of(quarter)
    rows, cells = part_ref.shape
    tiles = cells // 128
    features = out_ref.shape[0] // tiles
    levels = features // 3

    def store_rows(first, values):
        for tile in range(tiles):
            out_ref[pl.ds(first * tiles + tile, values.shape[0], stride=tiles), :] = values[
                :, tile * 128 : (tile + 1) * 128
            ]

    @pl.when(slot == 0)
    def _():
        for group, kinds in enumerate(plan1):
            heat = from_message(received[kinds.index("H")][...], levels, tiles)
            store_rows(group * levels, heat)

    @pl.when(slot != 0)
    def _():
        halos = receive_halos(plan1, slot, received, rows).astype(bf16)
        store_rows(0, (part_ref[...] + dot(halos, matrix_ref[cells:, :]))[:features])


VMEM = pl.BlockSpec(memory_space=pltpu.VMEM)
HBM = pl.BlockSpec(memory_space=pltpu.HBM)


def call(kernel, name, out_shape, *args, hbm=0, scratch=(), flops=0, limit=16 << 20):
    size = sum(a.size * a.dtype.itemsize for a in args)
    args = [
        pltpu.with_memory_space_constraint(a, pltpu.HBM) if index < hbm else a
        for index, a in enumerate(args)
    ]
    return pl.pallas_call(
        kernel,
        out_shape=out_shape,
        in_specs=[HBM] * hbm + [VMEM] * (len(args) - hbm),
        out_specs=jax.tree.map(lambda _: VMEM, out_shape),
        scratch_shapes=scratch,
        compiler_params=pltpu.CompilerParams(vmem_limit_bytes=limit),
        cost_estimate=pl.CostEstimate(flops=flops, bytes_accessed=size, transcendentals=0),
        name=name,
    )(*args)


def exchange(plan, messages, quarter, blocks):
    def partner(group, block, step):
        slot, place = group // quarter, group % quarter
        kinds = [kinds[step] for kinds in plan]
        if slot == 0:
            return (kinds.index("H") + 1) * quarter + place, block
        kind = kinds[slot - 1]
        if kind == "H":
            return place, block
        return group, (block + (1 if kind == "U" else -1)) % blocks

    received = []
    for step, message in enumerate(messages):
        pairs = []
        for group in range(4 * quarter):
            for block in range(blocks):
                to_group, to_block = partner(group, block, step)
                pairs.append((group * blocks + block, to_group * blocks + to_block))
        received.append(lax.ppermute(message, ("grp", "blk"), pairs))
    return received


def body(held, neighbours, send_rows, diffusion, transport, w_in, b_in, w_mid, b_mid, w_out, b_out):
    quarter, blocks = lax.axis_size("grp") // 4, lax.axis_size("blk")
    _, fields, levels, cells = held.shape
    halo, hidden = send_rows.shape[1], w_mid.shape[0]
    features, tiles = fields * levels, cells // 128
    rows = -(-features // 16) * 16
    length = -(-(max(levels * tiles, rows) + 8) // 16) * 16

    def shape(*dims, dtype=f32):
        return jax.ShapeDtypeStruct(dims, dtype)

    def like(array):
        return shape(*array.shape, dtype=array.dtype)

    message = shape(length, 128, dtype=i16)
    full = shape(rows, cells)
    matrix_shape = shape(cells + 2 * halo, cells, dtype=bf16)
    count0, count1 = len(plan0[0]), len(plan1[0])
    args = (neighbours, diffusion, transport, b_in[None], b_mid[None], b_out[None])
    *messages, flat, _, near, diff, tran, b_in, b_mid, b_out, pick = call(
        lambda *refs: pack_kernel(quarter, features, *refs), "pack",
        [message] * len(plan0[0])
        + [shape(rows * tiles, 128), like(send_rows)]
        + [like(array) for array in args]
        + [shape(cells, 2 * halo, dtype=bf16)],
        held.reshape(features * tiles, 128), send_rows, *args,
        hbm=2 + len(args), scratch=[pltpu.SemaphoreType.DMA((2 + len(args),))],
    )
    received = exchange(plan0, messages, quarter, blocks)
    matrix, matrix_low, keep, part1, w_in, c_in, c_mid, c_out, w_mid, w_out = call(
        lambda *refs: first_kernel(quarter, *refs), "first",
        [
            matrix_shape, matrix_shape, shape(1, cells), full,
            shape(hidden, rows, dtype=bf16), shape(hidden, 128), shape(hidden, 128), shape(levels, 128),
            like(w_mid), like(w_out),
        ],
        w_in.T, w_mid, w_out, flat, near, diff, tran, b_in, b_mid, b_out,
        hbm=3, scratch=[pltpu.VMEM((features, hidden), bf16), pltpu.SemaphoreType.DMA((3,))],
        flops=2 * cells * hidden * hidden,
    )
    weights = (w_in, c_in, w_mid, c_mid, w_out, c_out)
    *messages, state1 = call(
        lambda *refs: middle_kernel(
            quarter, refs[:count0], *refs[count0 : count0 + 10], refs[count0 + 10 : -1], refs[-1]
        ),
        "middle", [message] * count1 + [full],
        *received, pick, part1, matrix, matrix_low, *weights, flops=2 * cells * hidden * hidden,
    )
    received = exchange(plan1, messages, quarter, blocks)
    part2 = call(
        lambda *refs: own_kernel(quarter, *refs), "own", full, flat, state1, matrix, keep, *weights, flops=2 * cells * hidden * hidden
    )
    out = call(
        lambda *refs: last_kernel(quarter, refs[:count1], *refs[count1:]), "last",
        shape(features * tiles, 128), *received, part2, matrix, flops=2 * rows * cells * 2 * halo,
    )
    return out.reshape(held.shape)


def solution(mesh):
    placed = (
        P("grp", None, None, "blk"),
        P(None, "blk"),
        P(None, "blk"),
        P(None, "blk"),
        P(None, "blk"),
        P(),
        P(),
        P(),
        P(),
        P(),
        P(),
    )
    return jax.shard_map(
        body, mesh=mesh, in_specs=placed, out_specs=P("grp", None, None, "blk"), check_vma=False
    )
```
